32 devices in a mesh: blk: 8 (over z, y), shard: 4 (over x, core).
Axes of the slice: x: 2, y: 2, z: 4, core: 2. Of those that a mesh axis runs over, the one named last changes fastest.
Arguments:
- weights: bfloat16 [8, 8192, 2048], P('blk', 'shard'), may hold values from -90 to 90
- warm_factor: float32 [8, 32, 2048], P('blk'), may hold values from -6 to 6
Outputs:
- new_weights: bfloat16 [8, 8192, 2048], P('blk', 'shard')
- new_factor: float32 [8, 32, 2048], P('blk', None, 'shard')
The draws below stay inside these ranges and needn't reach their ends.
All inputs are finite; a program needn't handle non-finite values.
Results may differ from the reference program's by a relative error of at most 0.012.
Values may be sent and summed in bfloat16 or wider, within the bound.
No kernel may reach another device: no remote copies, remote signals or barrier semaphores. Data moves between devices by JAX's collectives and lax.ppermute only.
A program may use at most 64 MiB of HBM per device.

```python
from functools import partial
import jax
import jax.numpy as jnp
from jax import lax

HID = 8192
WID = 2048
RANK = 32
POWER = 4
REPLICAS = 8


def draw_weights(key, part):
    components = 3 * RANK // 2
    falloff = jnp.exp(jnp.log(0.25) / (RANK // 2) * jnp.arange(components, dtype=jnp.float32))
    row_place = jnp.arange(HID, dtype=jnp.float32) / HID
    roughness = jnp.exp(jax.random.uniform(jax.random.fold_in(key, 11), (HID,), minval=0.0, maxval=jnp.log(10.0)))
    row_scale = jnp.exp(jnp.log(3.0) * row_place) * roughness / 4.0
    left_vectors = jax.random.truncated_normal(jax.random.fold_in(key, 21), -3.0, 3.0, (REPLICAS, components, HID))
    right_vectors = jax.random.truncated_normal(jax.random.fold_in(key, 22), -3.0, 3.0, (REPLICAS, components, WID))
    amplitude = 0.44
    common_part = jnp.zeros((1, HID, WID), jnp.float32)
    noise = 0.25 * jax.random.truncated_normal(jax.random.fold_in(key, 13), -4.0, 4.0, (REPLICAS, HID, WID))
    weighted = left_vectors * (amplitude * falloff)[None, :, None]
    structured = jnp.einsum('rkh,rkw->rhw', weighted, right_vectors)
    values = (common_part + structured + noise) * row_scale[None, :, None]
    return jnp.clip(values, -90.0, 90.0).astype(jnp.bfloat16)


def shard_levels(own_key, shape, cuts, low, largest):
    factor_of = 1.0
    for dim, parts in cuts:
        draws = jax.random.uniform(jax.random.fold_in(jax.random.fold_in(own_key, 6), dim), (parts,), jnp.float32, low / len(cuts), largest / len(cuts))
        factor_of = factor_of * jnp.repeat(jnp.exp(draws), shape[dim] // parts).reshape((-1,) + (1,) * (len(shape) - 1 - dim))
    return factor_of


def gaussian(own_key, dims, width, limit, pieces=(), kind=jnp.bfloat16):
    loudness = shard_levels(own_key, dims, pieces, -0.22, 0.18) if pieces else 1.0
    entries = jax.random.normal(own_key, dims, jnp.float32) * width * loudness
    return jnp.minimum(jnp.maximum(entries, -limit), limit).astype(kind)


def setup_inputs(seed: int = 0) -> dict:
    arg_keys = jax.random.split(jax.random.key(seed), 3)
    weights = draw_weights(jax.random.fold_in(arg_keys[2], 71), 0)
    warm_factor = gaussian(arg_keys[1], (REPLICAS, RANK, WID), 1.0, 6.0, ((0, 8),), jnp.float32)
    return dict(weights=weights, warm_factor=warm_factor)


MIXING = 1.0 / 3.0

def power_edge(weights, arguments):
    edge_index, factor = arguments
    following = jnp.remainder(edge_index + 1, REPLICAS).astype(jnp.int32)
    lower_weight = lax.dynamic_index_in_dim(weights, edge_index.astype(jnp.int32), 0, keepdims=False)
    upper_weight = lax.dynamic_index_in_dim(weights, following, 0, keepdims=False)
    difference = lower_weight.astype(jnp.float32) - upper_weight.astype(jnp.float32)
    basis_rounded = jnp.zeros((RANK, HID), jnp.bfloat16)
    for iteration in range(POWER):
        rounded = lax.optimization_barrier(factor.astype(jnp.bfloat16))
        raw_factor = jnp.dot(rounded.astype(jnp.float32), difference.T, precision=lax.Precision.HIGHEST)
        gram = jnp.dot(raw_factor, raw_factor.T, precision=lax.Precision.HIGHEST)
        lower_factor = jnp.linalg.cholesky(gram)
        basis = jax.scipy.linalg.solve_triangular(lower_factor, raw_factor, lower=True)
        basis_rounded = lax.optimization_barrier(basis.astype(jnp.bfloat16))
        factor = jnp.dot(basis_rounded.astype(jnp.float32), difference, precision=lax.Precision.HIGHEST)
    return (basis_rounded, factor)

def reference(weights, warm_factor):
    edges = jnp.arange(REPLICAS, dtype=jnp.int32)
    bases, factors = lax.map(partial(power_edge, weights), (edges, warm_factor))
    final_rounded = factors.astype(jnp.bfloat16)

    def update(replica):
        prior = jnp.remainder(replica - 1 + REPLICAS, REPLICAS).astype(jnp.int32)
        replica = replica.astype(jnp.int32)
        signed = jnp.concatenate([lax.dynamic_index_in_dim(bases, prior, 0, keepdims=False), -lax.dynamic_index_in_dim(bases, replica, 0, keepdims=False)], axis=0)
        factor_pair = jnp.concatenate([lax.dynamic_index_in_dim(final_rounded, prior, 0, keepdims=False), lax.dynamic_index_in_dim(final_rounded, replica, 0, keepdims=False)], axis=0)
        delta = jnp.dot(signed.T.astype(jnp.float32), factor_pair.astype(jnp.float32), preferred_element_type=jnp.float32)
        own_weight = lax.dynamic_index_in_dim(weights, replica, 0, keepdims=False)
        return (own_weight.astype(jnp.float32) + MIXING * delta).astype(jnp.bfloat16)
    new_weights = lax.map(update, edges)
    return (new_weights, factors)
```

```python
import functools

import jax
import jax.numpy as jnp
from jax import lax
from jax.experimental import pallas as pl
from jax.experimental.pallas import tpu as pltpu
from jax.sharding import PartitionSpec as P

POWER = 4
MIXING = 1.0 / 3.0
LANES = 128
F32 = jnp.float32
BF16 = jnp.bfloat16
HIGHEST = lax.Precision.HIGHEST
VMEM = pl.BlockSpec(memory_space=pltpu.VMEM)
SMEM = pl.BlockSpec(memory_space=pltpu.SMEM)
HBM = pl.BlockSpec(memory_space=pl.ANY)


def kernel_call(body, outs, name, *operands, scratch=(), mib=8, flops=0, moved=0):
    specs = []
    for operand in operands:
        specs.append(SMEM if operand.dtype == jnp.int32 else VMEM)
    return pl.pallas_call(
        body,
        out_shape=outs,
        in_specs=specs,
        out_specs=jax.tree.map(lambda _: VMEM, outs),
        scratch_shapes=list(scratch),
        compiler_params=pltpu.CompilerParams(vmem_limit_bytes=mib * 1024 * 1024),
        cost_estimate=pl.CostEstimate(flops=flops, bytes_accessed=moved, transcendentals=0),
        name=name,
    )(*operands)


def out(shape, dtype):
    return jax.ShapeDtypeStruct(shape, dtype)


def hold_kernel(source, held, sem):
    copy = pltpu.make_async_copy(source, held, sem)
    copy.start()
    copy.wait()


def hold(weight):
    return pl.pallas_call(
        hold_kernel,
        out_shape=pltpu.VMEM(weight.shape, weight.dtype),
        in_specs=[HBM],
        out_specs=VMEM,
        scratch_shapes=[pltpu.SemaphoreType.DMA],
        compiler_params=pltpu.CompilerParams(vmem_limit_bytes=1024 * 1024),
        name="hold",
    )(weight)


def project(factor, weight, even, odd):
    rank = even.shape[0]
    product = lax.dot_general(
        factor, weight[...], (((1,), (1,)), ((), ())), preferred_element_type=F32
    )
    even[...] = product[:rank]
    odd[...] = product[rank:]


def first_kernel(place, own, prior, weight, even, odd, factor):
    rank = own.shape[0]
    parity = place[1]
    factor[pl.ds(pl.multiple_of(parity * rank, rank), rank), :] = own[...]
    factor[pl.ds(pl.multiple_of((1 - parity) * rank, rank), rank), :] = prior[...]
    project(factor[...], weight, even, odd)


def gathered(place, pieces, factor):
    width = pieces[0].shape[1]
    for offset, piece in enumerate(pieces):
        start = pl.multiple_of(jnp.bitwise_xor(place[0], offset) * width, width)
        factor[:, pl.ds(start, width)] = piece[...]


def next_kernel(place, *refs):
    *pieces, weight, even, odd, factor = refs
    gathered(place, pieces, factor)
    project(factor[...], weight, even, odd)


def back_kernel(slices, place, even, odd, even_other, odd_other, weight, keep, send, raw, total):
    rank, rows = even.shape
    width = weight.shape[1] // slices
    raw[:rank, :] = even[...] - even_other[...]
    raw[rank:, :] = odd[...] - odd_other[...]
    value = raw[...]
    high = value.astype(BF16)
    low = (value - high.astype(F32)).astype(BF16)
    both = jnp.dot(jnp.concatenate([high, low], axis=0), weight[...], preferred_element_type=F32)
    total[...] = both[: 2 * rank] + both[2 * rank :]
    mine = jnp.bitwise_and(place[0], 1)
    half = slices // 2
    for i in range(half):
        kept = pl.multiple_of((2 * i + mine) * width, width)
        sent = pl.multiple_of((2 * i + 1 - mine) * width, width)
        keep[:, i * width : (i + 1) * width] = total[:, pl.ds(kept, width)]
        send[:, i * width : (i + 1) * width] = total[:, pl.ds(sent, width)]
    product = lax.dot_general(
        value, value, (((1,), (1,)), ((), ())), precision=HIGHEST, preferred_element_type=F32
    )
    gram = jnp.concatenate([product[:rank, :rank], product[rank:, rank:]], axis=0)
    gram = jnp.concatenate([gram, jnp.zeros((2 * rank, LANES - rank), F32)], axis=1)
    keep[:, half * width :] = gram
    send[:, half * width :] = gram


def merge_kernel(bit, slices, place, held, came, keep, send):
    width = (held.shape[1] - LANES) // slices
    mine = jnp.bitwise_and(lax.div(place[0], jnp.int32(bit)), 1)
    for i in range(slices // 2):
        kept = pl.ds(pl.multiple_of((2 * i + mine) * width, width), width)
        sent = pl.ds(pl.multiple_of((2 * i + 1 - mine) * width, width), width)
        keep[:, i * width : (i + 1) * width] = held[:, kept] + came[:, kept]
        send[:, i * width : (i + 1) * width] = held[:, sent] + came[:, sent]
    last = slices // 2 * width
    gram = held[:, slices * width :] + came[:, slices * width :]
    keep[:, last:] = gram
    send[:, last:] = gram


def split_kernel(held, came, even, odd, gram):
    rank, width = even.shape
    even[...] = held[:rank, :width] + came[:rank, :width]
    odd[...] = held[rank:, :width] + came[rank:, :width]
    gram[...] = held[:, width:] + came[:, width:]


def inverse_kernel(gram, inverse):
    rank = gram.shape[0] // 2
    shape = (2, rank, LANES)
    lane = lax.broadcasted_iota(jnp.int32, shape, 2)
    row = lax.broadcasted_iota(jnp.int32, shape, 1)
    work = gram[...].reshape(shape)
    work = jnp.where(lane < rank, work, jnp.where(lane - rank == row, 1.0, 0.0))
    for k in range(rank):
        pivot = work[:, k : k + 1, :]
        scaled = pivot / pivot[:, :, k : k + 1]
        column = jnp.where(row[:, :, :1] > k, work[:, :, k : k + 1], 0.0)
        work = work - column * scaled
    diagonal = jnp.sum(jnp.where(lane == row, work, 0.0), axis=2, keepdims=True)
    work = work / jnp.sqrt(diagonal)
    inverse[...] = work.reshape(2 * rank, LANES)[:, rank : 2 * rank]


def normalised(inverse, even, odd):
    rank = even.shape[0]
    return jnp.concatenate(
        [
            jnp.dot(inverse[:rank, :], even, precision=HIGHEST, preferred_element_type=F32),
            jnp.dot(inverse[rank:, :], odd, precision=HIGHEST, preferred_element_type=F32),
        ],
        axis=0,
    )


def round_kernel(inverse, even, odd, even_other, odd_other, rounded):
    value = normalised(inverse[...], even[...] + even_other[...], odd[...] + odd_other[...])
    rounded[...] = value.astype(BF16)


def final_kernel(place, inverse, even, odd, even_other, odd_other, rounded, own, value):
    rank = even.shape[0]
    value[...] = normalised(inverse[...], even[...] + even_other[...], odd[...] + odd_other[...])
    rounded[...] = value[...].astype(BF16)
    own[...] = value[pl.ds(pl.multiple_of(place[1] * rank, rank), rank), :]


def basis_kernel(inverse, even, odd, even_other, odd_other, columns):
    basis = normalised(inverse[...], even[...] - even_other[...], odd[...] - odd_other[...])
    columns[...] = basis.T.astype(BF16)


def update_kernel(place, columns, *refs):
    *pieces, weight, result, factor = refs

    @pl.when(pl.program_id(0) == 0)
    def _():
        gathered(place, pieces, factor)

    tile = result.shape[0]
    rows = pl.ds(pl.multiple_of(pl.program_id(0) * tile, tile), tile)
    delta = jnp.dot(columns[rows, :], factor[...], preferred_element_type=F32)
    result[...] = (weight[rows, :].astype(F32) - MIXING * delta).astype(BF16)


def swapped(value, axis, pairs):
    return lax.ppermute(value, axis, pairs)


def on_device(weights, warm_factor):
    peers = lax.axis_size("blk")
    shards = lax.axis_size("shard")
    shard = lax.axis_index("shard")
    parity = lax.rem(lax.axis_index("blk"), 2)
    place = jnp.stack([shard, parity]).astype(jnp.int32)
    even_pairs = [(i, i + 1 if i % 2 == 0 else i - 1) for i in range(peers)]
    odd_pairs = [(i, (i + 1) % peers if i % 2 else (i - 1) % peers) for i in range(peers)]
    bits = [1 << i for i in range(shards.bit_length() - 1)]
    across = {bit: [(i, i ^ bit) for i in range(shards)] for bit in bits}

    own = warm_factor[0].astype(BF16)
    rank, wid = own.shape
    prior = lax.ppermute(own, "blk", [(i, (i + 1) % peers) for i in range(peers)])
    weight = hold(weights[0])
    rows = weight.shape[0]
    width = wid // shards
    factor_scratch = [pltpu.VMEM((2 * rank, wid), BF16)]
    product_outs = (out((rank, rows), F32), out((rank, rows), F32))
    full_cost = dict(flops=4 * rank * rows * wid, moved=rows * wid * 2)

    products = kernel_call(
        first_kernel, product_outs, "first", place, own, prior, weight,
        scratch=factor_scratch, mib=16, **full_cost,
    )
    for iteration in range(POWER):
        even, odd = products
        even_other = swapped(even, "blk", even_pairs)
        odd_other = swapped(odd, "blk", odd_pairs)
        slices = shards
        part = (2 * rank, slices // 2 * width + LANES)
        keep, send = kernel_call(
            functools.partial(back_kernel, slices),
            (out(part, F32), out(part, F32)), "back",
            place, even, odd, even_other, odd_other, weight,
            scratch=[pltpu.VMEM((2 * rank, rows), F32), pltpu.VMEM((2 * rank, wid), F32)],
            mib=20, flops=8 * rank * rows * wid, moved=rows * wid * 2,
        )
        for bit in bits:
            came = swapped(send, "shard", across[bit])
            slices //= 2
            if slices == 1:
                break
            part = (2 * rank, slices // 2 * width + LANES)
            keep, send = kernel_call(
                functools.partial(merge_kernel, 2 * bit, slices),
                (out(part, F32), out(part, F32)), "merge", place, keep, came,
            )
        piece = (rank, width)
        even_sum, odd_sum, gram = kernel_call(
            split_kernel, (out(piece, F32), out(piece, F32), out((2 * rank, LANES), F32)),
            "split", keep, came,
        )
        even_sum_other = swapped(even_sum, "blk", even_pairs)
        odd_sum_other = swapped(odd_sum, "blk", odd_pairs)
        inverse = kernel_call(
            inverse_kernel, out((2 * rank, rank), F32), "inverse", gram, flops=1000000, moved=8 * 1024 * 1024,
        )
        sums = (even_sum, odd_sum, even_sum_other, odd_sum_other)
        rounded_out = out((2 * rank, width), BF16)
        if iteration < POWER - 1:
            rounded = kernel_call(round_kernel, rounded_out, "round", inverse, *sums)
        else:
            columns = kernel_call(
                basis_kernel, out((rows, 2 * rank), BF16), "basis",
                inverse, even, odd, even_other, odd_other, mib=16,
                flops=8 * rank * rank * rows, moved=8 * 1024 * 1024,
            )
            rounded, new_factor = kernel_call(
                final_kernel, (rounded_out, out(piece, F32)), "final", place, inverse, *sums,
                scratch=[pltpu.VMEM((2 * rank, width), F32)],
            )
        pieces = {0: rounded}
        for bit in reversed(bits):
            for offset in list(pieces):
                pieces[offset ^ bit] = swapped(pieces[offset], "shard", across[bit])
        pieces = [pieces[offset] for offset in range(shards)]
        if iteration < POWER - 1:
            products = kernel_call(
                next_kernel, product_outs, "next", place, *pieces, weight,
                scratch=factor_scratch, mib=16, **full_cost,
            )
    tile = min(256, rows)
    new_weight = pl.pallas_call(
        update_kernel,
        grid=(rows // tile,),
        out_shape=out((rows, wid), BF16),
        in_specs=[SMEM] + [VMEM] * (len(pieces) + 2),
        out_specs=pl.BlockSpec((tile, wid), lambda i: (i, 0)),
        scratch_shapes=factor_scratch,
        compiler_params=pltpu.CompilerParams(vmem_limit_bytes=20 * 1024 * 1024),
        name="update",
    )(place, columns, *pieces, weight)
    return (new_weight[None], new_factor[None])


def solution(mesh):
    placed = (P("blk", "shard", None), P("blk", None, None))
    return jax.shard_map(
        on_device,
        mesh=mesh,
        in_specs=placed,
        out_specs=(P("blk", "shard", None), P("blk", None, "shard")),
        check_vma=False,
    )
```

```python
import functools

import jax
import jax.numpy as jnp
from jax import lax
from jax.experimental import pallas as pl
from jax.experimental.pallas import tpu as pltpu
from jax.sharding import PartitionSpec as P

POWER = 4
MIXING = 1.0 / 3.0
LANES = 128
MIB = 1024 * 1024
F32 = jnp.float32
BF16 = jnp.bfloat16
HIGHEST = lax.Precision.HIGHEST
VMEM = pl.BlockSpec(memory_space=pltpu.VMEM)
SMEM = pl.BlockSpec(memory_space=pltpu.SMEM)
HBM = pl.BlockSpec(memory_space=pl.ANY)


def kernel_call(body, outs, name, *operands, scratch=(), mib=8, flops=0, moved=0):
    specs = []
    for operand in operands:
        specs.append(SMEM if operand.dtype == jnp.int32 else VMEM)
    return pl.pallas_call(
        body,
        out_shape=outs,
        in_specs=specs,
        out_specs=jax.tree.map(lambda _: VMEM, outs),
        scratch_shapes=list(scratch),
        compiler_params=pltpu.CompilerParams(vmem_limit_bytes=mib * MIB),
        cost_estimate=pl.CostEstimate(flops=flops, bytes_accessed=moved, transcendentals=0),
        name=name,
    )(*operands)


def out(shape, dtype):
    return jax.ShapeDtypeStruct(shape, dtype)


def hold_kernel(source, held, turned, sems):
    tile = source.shape[0] // sems.shape[0]
    spans = [slice(i * tile, (i + 1) * tile) for i in range(sems.shape[0])]
    copies = [
        pltpu.make_async_copy(source.at[span, :], held.at[span, :], sems.at[i])
        for i, span in enumerate(spans)
    ]
    for copy in copies:
        copy.start()
    for copy, span in zip(copies, spans):
        copy.wait()
        turned[:, span] = held[span, :].T


def hold(weight):
    rows, wid = weight.shape
    return pl.pallas_call(
        hold_kernel,
        out_shape=(pltpu.VMEM((rows, wid), weight.dtype), pltpu.VMEM((wid, rows), weight.dtype)),
        in_specs=[HBM],
        out_specs=(VMEM, VMEM),
        scratch_shapes=[pltpu.SemaphoreType.DMA((max(1, rows // 256),))],
        compiler_params=pltpu.CompilerParams(vmem_limit_bytes=32 * MIB),
        cost_estimate=pl.CostEstimate(flops=0, bytes_accessed=2 * rows * wid, transcendentals=0),
        name="hold",
    )(weight)


def project(factor, turned, even, odd):
    rank = even.shape[0]
    product = jnp.dot(factor, turned[...], preferred_element_type=F32)
    even[...] = product[:rank]
    odd[...] = product[rank:]


def first_kernel(place, own, prior, turned, even, odd, factor):
    rank = own.shape[0]
    parity = place[1]
    factor[pl.ds(pl.multiple_of(parity * rank, rank), rank), :] = own[...]
    factor[pl.ds(pl.multiple_of((1 - parity) * rank, rank), rank), :] = prior[...]
    project(factor[...], turned, even, odd)


def gathered(place, pieces, factor):
    width = pieces[0].shape[1]
    for offset, piece in enumerate(pieces):
        start = pl.multiple_of(jnp.bitwise_xor(place[0], offset) * width, width)
        factor[:, pl.ds(start, width)] = piece[...]


def next_kernel(place, *refs):
    *pieces, turned, even, odd, factor = refs
    gathered(place, pieces, factor)
    project(factor[...], turned, even, odd)


def half_product(wanted, slices, both, weight, result):
    rank2 = both.shape[0] // 2
    width = weight.shape[1] // slices
    for i in range(slices // 2):
        start = pl.multiple_of((2 * i + wanted) * width, width)
        product = jnp.dot(both[...], weight[:, pl.ds(start, width)], preferred_element_type=F32)
        result[:, i * width : (i + 1) * width] = product[:rank2] + product[rank2:]


def back_send_kernel(slices, place, even, odd, even_other, odd_other, weight, both, send):
    rank = even.shape[0]
    for slot, (mine, theirs) in enumerate(((even, even_other), (odd, odd_other))):
        raw = mine[...] - theirs[...]
        high = raw.astype(BF16)
        both[slot * rank : (slot + 1) * rank, :] = high
        both[(2 + slot) * rank : (3 + slot) * rank, :] = (raw - high.astype(F32)).astype(BF16)
    half_product(1 - jnp.bitwise_and(place[0], 1), slices, both, weight, send)
    parts = lax.dot_general(
        both[...], both[...], (((1,), (1,)), ((), ())), preferred_element_type=F32
    )
    parts = parts[: 2 * rank] + parts[2 * rank :]
    parts = parts[:, : 2 * rank] + parts[:, 2 * rank :]
    gram = jnp.concatenate([parts[:rank, :rank], parts[rank:, rank:]], axis=0)
    send[:, -LANES:] = jnp.concatenate([gram, jnp.zeros((2 * rank, LANES - rank), F32)], axis=1)


def back_keep_kernel(slices, place, both, weight, keep):
    half_product(jnp.bitwise_and(place[0], 1), slices, both, weight, keep)


def chosen(place, bit):
    return jnp.bitwise_and(lax.div(place[0], jnp.int32(bit)), 1)


def merge_kernel(bit, slices, place, held, held_gram, came, keep, gram, send):
    width = held.shape[1] // slices
    mine = chosen(place, bit)
    for i in range(slices // 2):
        kept = pl.ds(pl.multiple_of((2 * i + mine) * width, width), width)
        sent = pl.ds(pl.multiple_of((2 * i + 1 - mine) * width, width), width)
        keep[:, i * width : (i + 1) * width] = held[:, kept] + came[:, kept]
        send[:, i * width : (i + 1) * width] = held[:, sent] + came[:, sent]
    total = held_gram[:, -LANES:] + came[:, -LANES:]
    gram[...] = total
    send[:, -LANES:] = total


def part_kernel(bit, place, held, held_gram, came, even, odd, even_sent, odd_sent, gram, send):
    rank, width = even.shape
    mine = chosen(place, bit)
    kept = pl.ds(pl.multiple_of(mine * width, width), width)
    sent = pl.ds(pl.multiple_of((1 - mine) * width, width), width)
    even[...] = held[:rank, kept] + came[:rank, kept]
    odd[...] = held[rank:, kept] + came[rank:, kept]
    leaving = held[:, sent] + came[:, sent]
    even_sent[...] = leaving[:rank]
    odd_sent[...] = leaving[rank:]
    send[:, :width] = leaving
    total = held_gram[:, -LANES:] + came[:, -LANES:]
    gram[...] = total
    send[:, width:] = total


def inverse_kernel(gram, came, inverse):
    rank = gram.shape[0] // 2
    shape = (2, rank, LANES)
    lane = lax.broadcasted_iota(jnp.int32, shape, 2)
    row = lax.broadcasted_iota(jnp.int32, shape, 1)
    work = (gram[...] + came[:, -LANES:]).reshape(shape)
    work = jnp.where(lane < rank, work, jnp.where(lane - rank == row, 1.0, 0.0))
    for k in range(rank):
        pivot = work[:, k : k + 1, :]
        scaled = pivot / pivot[:, :, k : k + 1]
        column = jnp.where(row[:, :, :1] > k, work[:, :, k : k + 1], 0.0)
        work = work - column * scaled
    diagonal = jnp.sum(jnp.where(lane == row, work, 0.0), axis=2, keepdims=True)
    work = work / jnp.sqrt(diagonal)
    inverse[...] = work.reshape(2 * rank, LANES)[:, rank : 2 * rank]


def normalised(inverse, even, odd):
    rank = even.shape[0]
    return jnp.concatenate(
        [
            jnp.dot(inverse[:rank, :], even, precision=HIGHEST, preferred_element_type=F32),
            jnp.dot(inverse[rank:, :], odd, precision=HIGHEST, preferred_element_type=F32),
        ],
        axis=0,
    )


def summed(inverse, came, even, odd, even_pair, odd_pair, even_far, odd_far):
    rank, width = even.shape
    even_sum = (even[...] + came[:rank, :width]) + (even_pair[...] + even_far[...])
    odd_sum = (odd[...] + came[rank:, :width]) + (odd_pair[...] + odd_far[...])
    return normalised(inverse[...], even_sum, odd_sum)


def round_kernel(*refs):
    *sums, rounded = refs
    rounded[...] = summed(*sums).astype(BF16)


def final_kernel(place, *refs):
    *sums, rounded, own, value = refs
    value[...] = summed(*sums)
    rounded[...] = value[...].astype(BF16)
    rank = own.shape[0]
    own[...] = value[pl.ds(pl.multiple_of(place[1] * rank, rank), rank), :]


def basis_kernel(inverse, both, columns):
    rank2 = both.shape[0] // 2
    raw = both[:rank2, :].astype(F32) + both[rank2:, :].astype(F32)
    basis = normalised(inverse[...], raw[: rank2 // 2], raw[rank2 // 2 :])
    columns[...] = basis.T.astype(BF16)


def update_kernel(place, columns, *refs):
    *pieces, weight, result, factor, made, sems = refs
    gathered(place, pieces, factor)
    tile = made.shape[0] // sems.shape[0]
    copies = []
    for i in range(sems.shape[0]):
        span = slice(i * tile, (i + 1) * tile)
        delta = jnp.dot(columns[span, :], factor[...], preferred_element_type=F32)
        made[span, :] = (weight[span, :].astype(F32) - MIXING * delta).astype(BF16)
        copy = pltpu.make_async_copy(made.at[span, :], result.at[span, :], sems.at[i])
        copy.start()
        copies.append(copy)
    for copy in copies:
        copy.wait()


def on_device(weights, warm_factor):
    peers = lax.axis_size("blk")
    shards = lax.axis_size("shard")
    shard = lax.axis_index("shard")
    parity = lax.rem(lax.axis_index("blk"), 2)
    place = jnp.stack([shard, parity]).astype(jnp.int32)
    bits = [1 << i for i in range(shards.bit_length() - 1)]
    last = bits[-1]
    partner = {
        0: [i + 1 if i % 2 == 0 else i - 1 for i in range(peers)],
        1: [(i + 1) % peers if i % 2 else (i - 1) % peers for i in range(peers)],
    }

    def across(value, bit):
        return lax.ppermute(value, "shard", [(i, i ^ bit) for i in range(shards)])

    def paired(value, slot):
        return lax.ppermute(value, "blk", list(enumerate(partner[slot])))

    def far(value, slot):
        pairs = [
            (i * shards + j, k * shards + (j ^ last))
            for i, k in enumerate(partner[slot])
            for j in range(shards)
        ]
        return lax.ppermute(value, ("blk", "shard"), pairs)

    own = warm_factor[0].astype(BF16)
    rank, wid = own.shape
    prior = lax.ppermute(own, "blk", [(i, (i + 1) % peers) for i in range(peers)])
    weight, turned = hold(weights[0])
    rows = weight.shape[0]
    width = wid // shards
    factor_scratch = [pltpu.VMEM((2 * rank, wid), BF16)]
    product_outs = (out((rank, rows), F32), out((rank, rows), F32))
    full_cost = dict(flops=4 * rank * rows * wid, moved=rows * wid * 2)
    gram_out = out((2 * rank, LANES), F32)
    piece = out((rank, width), F32)

    products = kernel_call(
        first_kernel, product_outs, "first", place, own, prior, turned,
        scratch=factor_scratch, mib=8, **full_cost,
    )
    for iteration in range(POWER):
        even, odd = products
        even_other = paired(even, 0)
        odd_other = paired(odd, 1)
        slices = shards
        half = slices // 2 * width
        both, send = kernel_call(
            functools.partial(back_send_kernel, slices),
            (out((4 * rank, rows), BF16), out((2 * rank, half + LANES), F32)), "back_send",
            place, even, odd, even_other, odd_other, weight, mib=8, **full_cost,
        )
        keep = kernel_call(
            functools.partial(back_keep_kernel, slices), out((2 * rank, half), F32), "back_keep",
            place, both, weight, mib=8, **full_cost,
        )
        gram = send
        for bit in bits[:-1]:
            came = across(send, bit)
            slices //= 2
            if 2 * bit == last:
                even_sum, odd_sum, even_sent, odd_sent, gram, send = kernel_call(
                    functools.partial(part_kernel, last),
                    (piece, piece, piece, piece, gram_out, out((2 * rank, width + LANES), F32)),
                    "part", place, keep, gram, came,
                )
                break
            half = slices // 2 * width
            keep, gram, send = kernel_call(
                functools.partial(merge_kernel, 2 * bit, slices),
                (out((2 * rank, half), F32), gram_out, out((2 * rank, half + LANES), F32)),
                "merge", place, keep, gram, came,
            )
        came = across(send, last)
        sums = (
            came, even_sum, odd_sum, paired(even_sum, 0), paired(odd_sum, 1),
            far(even_sent, 0), far(odd_sent, 1),
        )
        inverse = kernel_call(
            inverse_kernel, out((2 * rank, rank), F32), "inverse", gram, came,
            flops=1000000, moved=8 * MIB,
        )
        rounded_out = out((2 * rank, width), BF16)
        if iteration < POWER - 1:
            rounded = kernel_call(round_kernel, rounded_out, "round", inverse, *sums)
        else:
            columns = kernel_call(
                basis_kernel, out((rows, 2 * rank), BF16), "basis", inverse, both,
                mib=8, flops=8 * rank * rank * rows, moved=2 * MIB,
            )
            rounded, new_factor = kernel_call(
                final_kernel, (rounded_out, piece), "final", place, inverse, *sums,
                scratch=[pltpu.VMEM((2 * rank, width), F32)],
            )
        pieces = {0: rounded}
        for bit in reversed(bits):
            for offset in list(pieces):
                pieces[offset ^ bit] = across(pieces[offset], bit)
        pieces = [pieces[offset] for offset in range(shards)]
        if iteration < POWER - 1:
            products = kernel_call(
                next_kernel, product_outs, "next", place, *pieces, turned,
                scratch=factor_scratch, mib=8, **full_cost,
            )
    new_weight = pl.pallas_call(
        update_kernel,
        out_shape=out((rows, wid), BF16),
        in_specs=[SMEM] + [VMEM] * (len(pieces) + 2),
        out_specs=HBM,
        scratch_shapes=factor_scratch
        + [pltpu.VMEM((rows, wid), BF16), pltpu.SemaphoreType.DMA((max(1, rows // 256),))],
        compiler_params=pltpu.CompilerParams(vmem_limit_bytes=16 * MIB),
        cost_estimate=pl.CostEstimate(
            flops=4 * rank * rows * wid, bytes_accessed=2 * rows * wid, transcendentals=0
        ),
        name="update",
    )(place, columns, *pieces, weight)
    return (new_weight[None], new_factor[None])


def solution(mesh):
    placed = (P("blk", "shard", None), P("blk", None, None))
    return jax.shard_map(
        on_device,
        mesh=mesh,
        in_specs=placed,
        out_specs=(P("blk", "shard", None), P("blk", None, "shard")),
        check_vma=False,
    )
```

```python
import functools

import jax
import jax.numpy as jnp
from jax import lax
from jax.experimental import pallas as pl
from jax.experimental.pallas import tpu as pltpu
from jax.sharding import PartitionSpec as P

POWER = 4
MIXING = 1.0 / 3.0
LANES = 128
MIB = 1024 * 1024
F32 = jnp.float32
BF16 = jnp.bfloat16
HIGHEST = lax.Precision.HIGHEST
VMEM = pl.BlockSpec(memory_space=pltpu.VMEM)
SMEM = pl.BlockSpec(memory_space=pltpu.SMEM)
HBM = pl.BlockSpec(memory_space=pl.ANY)


def kernel_call(body, outs, name, *operands, scratch=(), mib=8, flops=0, moved=0):
    specs = []
    for operand in operands:
        specs.append(SMEM if operand.dtype == jnp.int32 else VMEM)
    return pl.pallas_call(
        body,
        out_shape=outs,
        in_specs=specs,
        out_specs=jax.tree.map(lambda _: VMEM, outs),
        scratch_shapes=list(scratch),
        compiler_params=pltpu.CompilerParams(vmem_limit_bytes=mib * MIB),
        cost_estimate=pl.CostEstimate(flops=flops, bytes_accessed=moved, transcendentals=0),
        name=name,
    )(*operands)


def out(shape, dtype):
    return jax.ShapeDtypeStruct(shape, dtype)


def hold_kernel(source, held, turned, sems):
    tile = source.shape[0] // sems.shape[0]
    spans = [slice(i * tile, (i + 1) * tile) for i in range(sems.shape[0])]
    copies = [
        pltpu.make_async_copy(source.at[span, :], held.at[span, :], sems.at[i])
        for i, span in enumerate(spans)
    ]
    for copy in copies:
        copy.start()
    for copy, span in zip(copies, spans):
        copy.wait()
        turned[:, span] = held[span, :].T


def hold(weight):
    rows, wid = weight.shape
    return pl.pallas_call(
        hold_kernel,
        out_shape=(pltpu.VMEM((rows, wid), weight.dtype), pltpu.VMEM((wid, rows), weight.dtype)),
        in_specs=[HBM],
        out_specs=(VMEM, VMEM),
        scratch_shapes=[pltpu.SemaphoreType.DMA((max(1, rows // 256),))],
        compiler_params=pltpu.CompilerParams(vmem_limit_bytes=32 * MIB),
        cost_estimate=pl.CostEstimate(flops=0, bytes_accessed=2 * rows * wid, transcendentals=0),
        name="hold",
    )(weight)


CHUNKS = 2


def first_kernel(chunk, place, own, prior, turned, even, odd, factor):
    rank, rows = even.shape
    parity = place[1]
    factor[pl.ds(pl.multiple_of(parity * rank, rank), rank), :] = own[...]
    factor[pl.ds(pl.multiple_of((1 - parity) * rank, rank), rank), :] = prior[...]
    product = jnp.dot(
        factor[...], turned[:, chunk * rows : (chunk + 1) * rows], preferred_element_type=F32
    )
    even[...] = product[:rank]
    odd[...] = product[rank:]


def slice_starts(place, offset, count, width, wid):
    low = jnp.bitwise_xor(jnp.bitwise_and(place[0], count - 1), offset) * width
    return pl.multiple_of(low, width), pl.multiple_of(low + wid // 2, width)


def piece_product(place, offset, count, piece, turned, columns):
    width = piece.shape[1] // 2
    low, high = slice_starts(place, offset, count, width, turned.shape[0])
    return jnp.dot(
        piece[:, :width], turned[pl.ds(low, width), columns], preferred_element_type=F32
    ) + jnp.dot(piece[:, width:], turned[pl.ds(high, width), columns], preferred_element_type=F32)


def own_kernel(count, place, piece, turned, partial):
    partial[...] = piece_product(place, 0, count, piece, turned, slice(None))


def next_kernel(chunk, place, *refs):
    *pieces, partial, turned, even, odd = refs
    rank, rows = even.shape
    columns = slice(chunk * rows, (chunk + 1) * rows)
    product = partial[:, columns]
    for offset, piece in enumerate(pieces, 1):
        product += piece_product(place, offset, len(pieces) + 1, piece, turned, columns)
    even[...] = product[:rank]
    odd[...] = product[rank:]


def gathered(place, pieces, factor):
    width = pieces[0].shape[1] // 2
    for offset, piece in enumerate(pieces):
        low, high = slice_starts(place, offset, len(pieces), width, factor.shape[1])
        factor[:, pl.ds(low, width)] = piece[:, :width]
        factor[:, pl.ds(high, width)] = piece[:, width:]


def chosen(place, bit):
    return jnp.bitwise_and(lax.div(place[0], jnp.int32(bit)), 1)


def split_raw(even, odd, even_other, odd_other, both):
    rank = even.shape[0]
    for slot, (mine, theirs) in enumerate(((even, even_other), (odd, odd_other))):
        raw = mine[...] - theirs[...]
        high = raw.astype(BF16)
        both[slot * rank : (slot + 1) * rank, :] = high
        both[(2 + slot) * rank : (3 + slot) * rank, :] = (raw - high.astype(F32)).astype(BF16)


def gram_of(both):
    rank = both.shape[0] // 4
    parts = lax.dot_general(
        both[...], both[...], (((1,), (1,)), ((), ())), preferred_element_type=F32
    )
    parts = parts[: 2 * rank] + parts[2 * rank :]
    parts = parts[:, : 2 * rank] + parts[:, 2 * rank :]
    gram = jnp.concatenate([parts[:rank, :rank], parts[rank:, rank:]], axis=0)
    return jnp.concatenate([gram, jnp.zeros((2 * rank, LANES - rank), F32)], axis=1)


def folded(product):
    rank2 = product.shape[0] // 2
    return product[:rank2] + product[rank2:]


def back_kernel(chunk, *refs):
    *products, weight, both, total, gram = refs
    rows = both.shape[1]
    split_raw(*products, both)
    total[...] = folded(
        jnp.dot(
            both[...], weight[chunk * rows : (chunk + 1) * rows, :], preferred_element_type=F32
        )
    )
    gram[...] = gram_of(both)


def half_product(wanted, slices, both, total, weight, result):
    rows = both.shape[1]
    width = weight.shape[1] // slices
    for i in range(slices // 2):
        columns = pl.ds(pl.multiple_of((2 * i + wanted) * width, width), width)
        product = jnp.dot(
            both[...], weight[weight.shape[0] - rows :, columns], preferred_element_type=F32
        )
        result[:, i * width : (i + 1) * width] = total[:, columns] + folded(product)


def back_send_kernel(slices, place, *refs):
    *products, total, gram, weight, both, send = refs
    split_raw(*products, both)
    half_product(1 - chosen(place, 1), slices, both, total, weight, send)
    send[:, -LANES:] = gram[...] + gram_of(both)


def back_keep_kernel(slices, place, both, total, weight, keep):
    half_product(chosen(place, 1), slices, both, total, weight, keep)


def merge_kernel(bit, slices, place, held, held_gram, came, keep, send):
    width = held.shape[1] // slices
    mine = chosen(place, bit)
    for i in range(slices // 2):
        kept = pl.ds(pl.multiple_of((2 * i + mine) * width, width), width)
        sent = pl.ds(pl.multiple_of((2 * i + 1 - mine) * width, width), width)
        keep[:, i * width : (i + 1) * width] = held[:, kept] + came[:, kept]
        send[:, i * width : (i + 1) * width] = held[:, sent] + came[:, sent]
    send[:, -LANES:] = held_gram[:, -LANES:] + came[:, -LANES:]


def add_kernel(held, held_gram, came, even, odd, gram):
    rank = even.shape[0]
    even[...] = held[:rank, :] + came[:rank, :-LANES]
    odd[...] = held[rank:, :] + came[rank:, :-LANES]
    gram[...] = held_gram[:, -LANES:] + came[:, -LANES:]


def inverse_kernel(gram, came, inverse):
    rank = gram.shape[0] // 2
    shape = (2, rank, LANES)
    lane = lax.broadcasted_iota(jnp.int32, shape, 2)
    row = lax.broadcasted_iota(jnp.int32, shape, 1)
    work = (gram[...] + came[...]).reshape(shape)
    work = jnp.where(lane < rank, work, jnp.where(lane - rank == row, 1.0, 0.0))
    for k in range(rank):
        pivot = work[:, k : k + 1, :]
        scaled = pivot / pivot[:, :, k : k + 1]
        column = jnp.where(row[:, :, :1] > k, work[:, :, k : k + 1], 0.0)
        work = work - column * scaled
    diagonal = jnp.sum(jnp.where(lane == row, work, 0.0), axis=2, keepdims=True)
    work = work / jnp.sqrt(diagonal)
    inverse[...] = work.reshape(2 * rank, LANES)[:, rank : 2 * rank]


def normalised(inverse, even, odd):
    rank = even.shape[0]
    return jnp.concatenate(
        [
            jnp.dot(inverse[:rank, :], even, precision=HIGHEST, preferred_element_type=F32),
            jnp.dot(inverse[rank:, :], odd, precision=HIGHEST, preferred_element_type=F32),
        ],
        axis=0,
    )


def share_kernel(inverse, even, odd, even_pair, odd_pair, share):
    value = normalised(inverse[...], even[...] + even_pair[...], odd[...] + odd_pair[...])
    share[...] = value.astype(share.dtype)


def blend_kernel(share, came, rounded):
    rounded[...] = (share[...].astype(F32) + came[...].astype(F32)).astype(BF16)


def final_kernel(bit, place, share, came, rounded, own):
    rank, width = own.shape
    value = share[...] + came[...]
    rounded[...] = value.astype(BF16)
    rows = pl.ds(pl.multiple_of(place[1] * rank, rank), rank)
    columns = pl.ds(pl.multiple_of(chosen(place, bit) * width, width), width)
    own[...] = share[rows, columns] + came[rows, columns]


def basis_kernel(inverse, *refs):
    *chunks, columns = refs
    for i, both in enumerate(chunks):
        rank2 = both.shape[0] // 2
        rows = both.shape[1]
        raw = both[:rank2, :].astype(F32) + both[rank2:, :].astype(F32)
        basis = normalised(inverse[...], raw[: rank2 // 2], raw[rank2 // 2 :])
        columns[i * rows : (i + 1) * rows, :] = basis.T.astype(BF16)


def update_kernel(place, columns, *refs):
    *pieces, weight, result, factor, made, sems = refs
    gathered(place, pieces, factor)
    tile = made.shape[0] // sems.shape[0]
    copies = []
    for i in range(sems.shape[0]):
        span = slice(i * tile, (i + 1) * tile)
        delta = jnp.dot(columns[span, :], factor[...], preferred_element_type=F32)
        made[span, :] = (weight[span, :].astype(F32) - MIXING * delta).astype(BF16)
        copy = pltpu.make_async_copy(made.at[span, :], result.at[span, :], sems.at[i])
        copy.start()
        copies.append(copy)
    for copy in copies:
        copy.wait()


def on_device(weights, warm_factor):
    peers = lax.axis_size("blk")
    shards = lax.axis_size("shard")
    shard = lax.axis_index("shard")
    parity = lax.rem(lax.axis_index("blk"), 2)
    place = jnp.stack([shard, parity]).astype(jnp.int32)
    bits = [1 << i for i in range(shards.bit_length() - 1)]
    last = bits[-1]
    partner = {
        0: [i + 1 if i % 2 == 0 else i - 1 for i in range(peers)],
        1: [(i + 1) % peers if i % 2 else (i - 1) % peers for i in range(peers)],
    }

    def across(value, bit):
        return lax.ppermute(value, "shard", [(i, i ^ bit) for i in range(shards)])

    def paired(value, slot):
        return lax.ppermute(value, "blk", list(enumerate(partner[slot])))

    own = warm_factor[0].astype(BF16)
    rank, wid = own.shape
    prior = lax.ppermute(own, "blk", [(i, (i + 1) % peers) for i in range(peers)])
    weight, turned = hold(weights[0])
    rows = weight.shape[0]
    width = wid // shards
    chunk_rows = rows // CHUNKS
    cost = dict(flops=4 * rank * chunk_rows * wid, moved=chunk_rows * wid * 2)
    product_outs = (out((rank, chunk_rows), F32), out((rank, chunk_rows), F32))
    factor_scratch = [pltpu.VMEM((2 * rank, wid), BF16)]
    gram_out = out((2 * rank, LANES), F32)
    both_out = out((4 * rank, chunk_rows), BF16)
    part_out = out((rank, 2 * width), F32)

    products = [
        kernel_call(
            functools.partial(first_kernel, chunk), product_outs, "first",
            place, own, prior, turned, scratch=factor_scratch, mib=8, **cost,
        )
        for chunk in range(CHUNKS)
    ]
    for iteration in range(POWER):
        final = iteration == POWER - 1
        exchanged = [
            [*pair, *(paired(product, slot) for slot, product in enumerate(pair))]
            for pair in products
        ]
        slices = shards
        half = slices // 2 * width
        both, total, gram = kernel_call(
            functools.partial(back_kernel, 0), (both_out, out((2 * rank, wid), F32), gram_out),
            "back", *exchanged[0], weight, mib=8, **cost,
        )
        both_last, send = kernel_call(
            functools.partial(back_send_kernel, slices),
            (both_out, out((2 * rank, half + LANES), F32)), "back_send",
            place, *exchanged[1], total, gram, weight, mib=8, **cost,
        )
        keep = kernel_call(
            functools.partial(back_keep_kernel, slices), out((2 * rank, half), F32), "back_keep",
            place, both_last, total, weight, mib=8, **cost,
        )
        gram = send
        for bit in bits[:-1]:
            came = across(send, bit)
            slices //= 2
            half = slices // 2 * width
            if 2 * bit == last:
                even, odd, gram = kernel_call(
                    add_kernel, (part_out, part_out, gram_out), "add", keep, gram, came
                )
                break
            keep, send = kernel_call(
                functools.partial(merge_kernel, 2 * bit, slices),
                (out((2 * rank, half), F32), out((2 * rank, half + LANES), F32)), "merge",
                place, keep, gram, came,
            )
            gram = send
        gram_came = across(gram, last)
        pair = (paired(even, 0), paired(odd, 1))
        inverse = kernel_call(
            inverse_kernel, out((2 * rank, rank), F32), "inverse", gram, gram_came,
            flops=1000000, moved=8 * MIB,
        )
        share = kernel_call(
            share_kernel, out((2 * rank, 2 * width), F32 if final else BF16), "share",
            inverse, even, odd, *pair,
        )
        came = across(share, last)
        rounded_out = out((2 * rank, 2 * width), BF16)
        if final:
            columns = kernel_call(
                basis_kernel, out((rows, 2 * rank), BF16), "basis", inverse, both, both_last,
                mib=8, flops=8 * rank * rank * rows, moved=2 * MIB,
            )
            rounded, new_factor = kernel_call(
                functools.partial(final_kernel, last), (rounded_out, out((rank, width), F32)),
                "final", place, share, came,
            )
        else:
            rounded = kernel_call(blend_kernel, rounded_out, "blend", share, came)
        pieces = {0: rounded}
        for bit in reversed(bits[:-1]):
            for offset in list(pieces):
                pieces[offset ^ bit] = across(pieces[offset], bit)
        pieces = [pieces[offset] for offset in range(last)]
        if not final:
            partial = kernel_call(
                functools.partial(own_kernel, last), out((2 * rank, rows), F32), "own",
                place, rounded, turned, mib=8, **cost,
            )
            products = [
                kernel_call(
                    functools.partial(next_kernel, chunk), product_outs, "next",
                    place, *pieces[1:], partial, turned, mib=8, **cost,
                )
                for chunk in range(CHUNKS)
            ]
    new_weight = pl.pallas_call(
        update_kernel,
        out_shape=out((rows, wid), BF16),
        in_specs=[SMEM] + [VMEM] * (len(pieces) + 2),
        out_specs=HBM,
        scratch_shapes=[*factor_scratch, pltpu.VMEM((rows, wid), BF16), pltpu.SemaphoreType.DMA((max(1, rows // 256),))],
        compiler_params=pltpu.CompilerParams(vmem_limit_bytes=16 * MIB),
        cost_estimate=pl.CostEstimate(
            flops=4 * rank * rows * wid, bytes_accessed=2 * rows * wid, transcendentals=0
        ),
        name="update",
    )(place, columns, *pieces, weight)
    return (new_weight[None], new_factor[None])


def solution(mesh):
    placed = (P("blk", "shard", None), P("blk", None, None))
    return jax.shard_map(
        on_device,
        mesh=mesh,
        in_specs=placed,
        out_specs=(P("blk", "shard", None), P("blk", None, "shard")),
        check_vma=False,
    )
```

```python
import functools

import jax
import jax.numpy as jnp
from jax import lax
from jax.experimental import pallas as pl
from jax.experimental.pallas import tpu as pltpu
from jax.sharding import PartitionSpec as P

POWER = 4
MIXING = 1.0 / 3.0
CHUNKS = 2
LANES = 128
PIVOTS = 4
MIB = 1024 * 1024
F32 = jnp.float32
BF16 = jnp.bfloat16
HIGHEST = lax.Precision.HIGHEST
VMEM = pl.BlockSpec(memory_space=pltpu.VMEM)
SMEM = pl.BlockSpec(memory_space=pltpu.SMEM)
HBM = pl.BlockSpec(memory_space=pl.ANY)


def kernel_call(body, outs, name, *operands, scratch=(), mib=8, flops=0, moved=0):
    specs = []
    for operand in operands:
        specs.append(SMEM if operand.dtype == jnp.int32 else VMEM)
    return pl.pallas_call(
        body,
        out_shape=outs,
        in_specs=specs,
        out_specs=jax.tree.map(lambda _: VMEM, outs),
        scratch_shapes=list(scratch),
        compiler_params=pltpu.CompilerParams(vmem_limit_bytes=mib * MIB),
        cost_estimate=pl.CostEstimate(flops=flops, bytes_accessed=moved, transcendentals=0),
        name=name,
    )(*operands)


def out(shape, dtype):
    return jax.ShapeDtypeStruct(shape, dtype)


def hold_kernel(source, held, turned, sems):
    tile = source.shape[0] // sems.shape[0]
    spans = [slice(i * tile, (i + 1) * tile) for i in range(sems.shape[0])]
    copies = [
        pltpu.make_async_copy(source.at[span, :], held.at[span, :], sems.at[i])
        for i, span in enumerate(spans)
    ]
    for copy in copies:
        copy.start()
    for copy, span in zip(copies, spans):
        copy.wait()
        turned[:, span] = held[span, :].T


def hold(weight):
    rows, wid = weight.shape
    return pl.pallas_call(
        hold_kernel,
        out_shape=(pltpu.VMEM((rows, wid), weight.dtype), pltpu.VMEM((wid, rows), weight.dtype)),
        in_specs=[HBM],
        out_specs=(VMEM, VMEM),
        scratch_shapes=[pltpu.SemaphoreType.DMA((max(1, rows // 256),))],
        compiler_params=pltpu.CompilerParams(vmem_limit_bytes=32 * MIB),
        cost_estimate=pl.CostEstimate(flops=0, bytes_accessed=2 * rows * wid, transcendentals=0),
        name="hold",
    )(weight)


def first_kernel(chunk, place, own, prior, turned, even, odd, factor):
    rank, rows = even.shape
    parity = place[1]
    factor[pl.ds(pl.multiple_of(parity * rank, rank), rank), :] = own[...]
    factor[pl.ds(pl.multiple_of((1 - parity) * rank, rank), rank), :] = prior[...]
    product = jnp.dot(
        factor[...], turned[:, chunk * rows : (chunk + 1) * rows], preferred_element_type=F32
    )
    even[...] = product[:rank]
    odd[...] = product[rank:]


def slice_starts(place, offset, count, width, wid):
    low = jnp.bitwise_xor(jnp.bitwise_and(place[0], count - 1), offset) * width
    return pl.multiple_of(low, width), pl.multiple_of(low + wid // 2, width)


def piece_product(place, offset, count, piece, turned, columns):
    width = piece.shape[1] // 2
    low, high = slice_starts(place, offset, count, width, turned.shape[0])
    return jnp.dot(
        piece[:, :width], turned[pl.ds(low, width), columns], preferred_element_type=F32
    ) + jnp.dot(piece[:, width:], turned[pl.ds(high, width), columns], preferred_element_type=F32)


def own_kernel(count, place, piece, turned, partial):
    partial[...] = piece_product(place, 0, count, piece, turned, slice(None))


def next_kernel(chunk, place, *refs):
    *pieces, partial, turned, even, odd = refs
    rank, rows = even.shape
    columns = slice(chunk * rows, (chunk + 1) * rows)
    product = partial[:, columns]
    for offset, piece in enumerate(pieces, 1):
        product += piece_product(place, offset, len(pieces) + 1, piece, turned, columns)
    even[...] = product[:rank]
    odd[...] = product[rank:]


def chosen(place, bit):
    return jnp.bitwise_and(lax.div(place[0], jnp.int32(bit)), 1)


def split_raw(even, odd, even_other, odd_other, both):
    rank = even.shape[0]
    for slot, (mine, theirs) in enumerate(((even, even_other), (odd, odd_other))):
        raw = mine[...] - theirs[...]
        high = raw.astype(BF16)
        both[slot * rank : (slot + 1) * rank, :] = high
        both[(2 + slot) * rank : (3 + slot) * rank, :] = (raw - high.astype(F32)).astype(BF16)


def gram_of(both):
    rank = both.shape[0] // 4
    parts = lax.dot_general(
        both[...], both[...], (((1,), (1,)), ((), ())), preferred_element_type=F32
    )
    parts = parts[: 2 * rank] + parts[2 * rank :]
    parts = parts[:, : 2 * rank] + parts[:, 2 * rank :]
    gram = jnp.concatenate([parts[:rank, :rank], parts[rank:, rank:]], axis=0)
    return jnp.concatenate([gram, jnp.zeros((2 * rank, LANES - rank), F32)], axis=1)


def folded(product):
    rank2 = product.shape[0] // 2
    return product[:rank2] + product[rank2:]


def back_kernel(chunk, *refs):
    *products, weight, both, total, gram = refs
    rows = both.shape[1]
    split_raw(*products, both)
    total[...] = folded(
        jnp.dot(
            both[...], weight[chunk * rows : (chunk + 1) * rows, :], preferred_element_type=F32
        )
    )
    gram[...] = gram_of(both)


def half_product(wanted, slices, both, total, weight, result):
    rows = both.shape[1]
    width = weight.shape[1] // slices
    for i in range(slices // 2):
        columns = pl.ds(pl.multiple_of((2 * i + wanted) * width, width), width)
        product = jnp.dot(
            both[...], weight[weight.shape[0] - rows :, columns], preferred_element_type=F32
        )
        result[:, i * width : (i + 1) * width] = total[:, columns] + folded(product)


def back_send_kernel(slices, place, *refs):
    *products, total, gram, weight, both, send = refs
    split_raw(*products, both)
    half_product(1 - chosen(place, 1), slices, both, total, weight, send)
    send[:, -LANES:] = gram[...] + gram_of(both)


def back_keep_kernel(slices, place, both, total, weight, keep):
    half_product(chosen(place, 1), slices, both, total, weight, keep)


def merge_kernel(bit, slices, place, held, held_gram, came, keep, send):
    width = held.shape[1] // slices
    mine = chosen(place, bit)
    for i in range(slices // 2):
        kept = pl.ds(pl.multiple_of((2 * i + mine) * width, width), width)
        sent = pl.ds(pl.multiple_of((2 * i + 1 - mine) * width, width), width)
        keep[:, i * width : (i + 1) * width] = held[:, kept] + came[:, kept]
        send[:, i * width : (i + 1) * width] = held[:, sent] + came[:, sent]
    send[:, -LANES:] = held_gram[:, -LANES:] + came[:, -LANES:]


def add_kernel(held, held_gram, came, even, odd, gram):
    rank = even.shape[0]
    even[...] = held[:rank, :] + came[:rank, :-LANES]
    odd[...] = held[rank:, :] + came[rank:, :-LANES]
    gram[...] = held_gram[:, -LANES:] + came[:, -LANES:]


def inverse_kernel(gram, came, inverse):
    rank = gram.shape[0] // 2
    shape = (2, rank, LANES)
    lane = lax.broadcasted_iota(jnp.int32, shape, 2)
    row = lax.broadcasted_iota(jnp.int32, shape, 1)
    work = (gram[...] + came[...]).reshape(shape)
    work = jnp.where(lane < rank, work, jnp.where(lane - rank == row, 1.0, 0.0))
    for k in range(0, rank, PIVOTS):
        span = range(k, min(k + PIVOTS, rank))
        columns = [jnp.broadcast_to(work[:, :, j : j + 1], shape) for j in span]
        for i, j in enumerate(span):
            scale = 1.0 / columns[i][:, j : j + 1, :]
            below = jnp.where(row > j, columns[i], 0.0)
            work = work - below * (work[:, j : j + 1, :] * scale)
            for later in range(i + 1, len(columns)):
                other = columns[later]
                columns[later] = other - below * (other[:, j : j + 1, :] * scale)
    diagonal = jnp.sum(jnp.where(lane == row, work, 0.0), axis=2, keepdims=True)
    work = work / jnp.sqrt(diagonal)
    inverse[...] = work.reshape(2 * rank, LANES)[:, rank : 2 * rank]


def normalised(inverse, even, odd):
    rank = even.shape[0]
    return jnp.concatenate(
        [
            jnp.dot(inverse[:rank, :], even, precision=HIGHEST, preferred_element_type=F32),
            jnp.dot(inverse[rank:, :], odd, precision=HIGHEST, preferred_element_type=F32),
        ],
        axis=0,
    )


def share_kernel(inverse, even, odd, even_pair, odd_pair, share):
    value = normalised(inverse[...], even[...] + even_pair[...], odd[...] + odd_pair[...])
    share[...] = value.astype(share.dtype)


def blend_kernel(share, came, *refs):
    refs[-1][...] = (share[...].astype(F32) + came[...].astype(F32)).astype(BF16)


def basis_kernel(inverse, *refs):
    *chunks, columns = refs
    for i, both in enumerate(chunks):
        rank2 = both.shape[0] // 2
        rows = both.shape[1]
        raw = both[:rank2, :].astype(F32) + both[rank2:, :].astype(F32)
        basis = normalised(inverse[...], raw[: rank2 // 2], raw[rank2 // 2 :])
        columns[i * rows : (i + 1) * rows, :] = basis.T.astype(BF16)


def updated(columns, piece, weight, rows, there, held):
    delta = jnp.dot(columns[rows, :], piece[:, held], preferred_element_type=F32)
    return (weight[rows, there].astype(F32) - MIXING * delta).astype(BF16)


def update_own_kernel(count, place, columns, piece, weight, made):
    rows, width = made.shape[1:]
    tile = min(512, rows)
    for j, start in enumerate(slice_starts(place, 0, count, width, weight.shape[1])):
        for first in range(0, rows, tile):
            span = slice(first, first + tile)
            held = slice(j * width, (j + 1) * width)
            made[j, span, :] = updated(columns, piece, weight, span, pl.ds(start, width), held)


def update_kernel(bit, count, place, columns, *refs):
    pieces = refs[: count - 1]
    own_made, share, came, weight, result, own, made, value, own_sem, sems = refs[count - 1 :]
    rank, width = own.shape
    mine = pl.ds(pl.multiple_of(chosen(place, bit) * width, width), width)
    ours = pl.ds(pl.multiple_of(place[1] * rank, rank), rank)
    value[...] = share[ours, mine] + came[ours, mine]
    copies = [pltpu.make_async_copy(value, own, own_sem)]
    copies[0].start()
    rows = weight.shape[0]

    def put(source, index, span, there):
        copy = pltpu.make_async_copy(source, result.at[span, there], sems.at[index])
        copy.start()
        copies.append(copy)

    index = 0
    for j, start in enumerate(slice_starts(place, 0, count, width, weight.shape[1])):
        put(own_made.at[j], index, slice(None), pl.ds(start, width))
        index += 1
    tile = rows // ((sems.shape[0] - 2) // (2 * (count - 1)))
    for i, piece in enumerate(pieces):
        for j, start in enumerate(slice_starts(place, i + 1, count, width, weight.shape[1])):
            there = pl.ds(start, width)
            held = slice(j * width, (j + 1) * width)
            for first in range(0, rows, tile):
                span = slice(first, first + tile)
                made[2 * i + j, span, :] = updated(columns, piece, weight, span, there, held)
                put(made.at[2 * i + j, span, :], index, span, there)
                index += 1
    for copy in copies:
        copy.wait()


def on_device(weights, warm_factor):
    peers = lax.axis_size("blk")
    shards = lax.axis_size("shard")
    shard = lax.axis_index("shard")
    parity = lax.rem(lax.axis_index("blk"), 2)
    place = jnp.stack([shard, parity]).astype(jnp.int32)
    bits = [1 << i for i in range(shards.bit_length() - 1)]
    last = bits[-1]
    partner = {
        0: [i + 1 if i % 2 == 0 else i - 1 for i in range(peers)],
        1: [(i + 1) % peers if i % 2 else (i - 1) % peers for i in range(peers)],
    }

    def across(value, bit):
        return lax.ppermute(value, "shard", [(i, i ^ bit) for i in range(shards)])

    def paired(value, slot):
        return lax.ppermute(value, "blk", list(enumerate(partner[slot])))

    own = warm_factor[0].astype(BF16)
    rank, wid = own.shape
    prior = lax.ppermute(own, "blk", [(i, (i + 1) % peers) for i in range(peers)])
    weight, turned = hold(weights[0])
    rows = weight.shape[0]
    width = wid // shards
    chunk_rows = rows // CHUNKS
    cost = dict(flops=4 * rank * chunk_rows * wid, moved=chunk_rows * wid * 2)
    product_outs = (out((rank, chunk_rows), F32), out((rank, chunk_rows), F32))
    factor_scratch = [pltpu.VMEM((2 * rank, wid), BF16)]
    gram_out = out((2 * rank, LANES), F32)
    both_out = out((4 * rank, chunk_rows), BF16)
    part_out = out((rank, 2 * width), F32)

    products = [
        kernel_call(
            functools.partial(first_kernel, chunk), product_outs, "first",
            place, own, prior, turned, scratch=factor_scratch, mib=8, **cost,
        )
        for chunk in range(CHUNKS)
    ]
    for iteration in range(POWER):
        final = iteration == POWER - 1
        even_other = paired(products[0][0], 0)
        odd_other = paired(products[0][1], 1)
        odd_last = paired(products[1][1], 1)
        even_last = paired(products[1][0], 0)
        exchanged = [(*products[0], even_other, odd_other), (*products[1], even_last, odd_last)]
        slices = shards
        half = slices // 2 * width
        both, total, gram = kernel_call(
            functools.partial(back_kernel, 0), (both_out, out((2 * rank, wid), F32), gram_out),
            "back", *exchanged[0], weight, mib=8, **cost,
        )
        both_last, send = kernel_call(
            functools.partial(back_send_kernel, slices),
            (both_out, out((2 * rank, half + LANES), F32)), "back_send",
            place, *exchanged[1], total, gram, weight, mib=8, **cost,
        )
        keep = kernel_call(
            functools.partial(back_keep_kernel, slices), out((2 * rank, half), F32), "back_keep",
            place, both_last, total, weight, mib=8, **cost,
        )
        gram = send
        for bit in bits[:-1]:
            came = across(send, bit)
            slices //= 2
            half = slices // 2 * width
            if 2 * bit == last:
                even, odd, gram = kernel_call(
                    add_kernel, (part_out, part_out, gram_out), "add", keep, gram, came
                )
                break
            keep, send = kernel_call(
                functools.partial(merge_kernel, 2 * bit, slices),
                (out((2 * rank, half), F32), out((2 * rank, half + LANES), F32)), "merge",
                place, keep, gram, came,
            )
            gram = send
        gram_came = across(gram, last)
        odd_pair = paired(odd, 1)
        even_pair = paired(even, 0)
        inverse = kernel_call(
            inverse_kernel, out((2 * rank, rank), F32), "inverse", gram, gram_came,
            flops=1000000, moved=8 * MIB,
        )
        share = kernel_call(
            share_kernel, out((2 * rank, 2 * width), F32 if final else BF16), "share",
            inverse, even, odd, even_pair, odd_pair,
        )
        came = across(share, last)
        if final:
            columns = kernel_call(
                basis_kernel, out((rows, 2 * rank), BF16), "basis", inverse, both, both_last,
                mib=8, flops=8 * rank * rank * rows, moved=2 * MIB,
            )
        rounded = kernel_call(
            blend_kernel, out((2 * rank, 2 * width), BF16), "blend",
            share, came, *([columns] if final else []),
        )
        pieces = {0: rounded}
        for bit in reversed(bits[:-1]):
            for offset in list(pieces):
                pieces[offset ^ bit] = across(pieces[offset], bit)
        pieces = [pieces[offset] for offset in range(last)]
        if not final:
            partial = kernel_call(
                functools.partial(own_kernel, last), out((2 * rank, rows), F32), "own",
                place, rounded, turned, mib=8, **cost,
            )
            products = [
                kernel_call(
                    functools.partial(next_kernel, chunk), product_outs, "next",
                    place, *pieces[1:], partial, turned, mib=8, **cost,
                )
                for chunk in range(CHUNKS)
            ]
    made = kernel_call(
        functools.partial(update_own_kernel, last), out((2, rows, width), BF16), "update_own",
        place, columns, rounded, weight, mib=8, flops=8 * rank * rows * width, moved=6 * rows * width,
    )
    tiles = max(1, rows // 512)
    new_weight, new_factor = pl.pallas_call(
        functools.partial(update_kernel, last, last),
        out_shape=(out((rows, wid), BF16), out((rank, width), F32)),
        in_specs=[SMEM] + [VMEM] * (last + 4),
        out_specs=(HBM, HBM),
        scratch_shapes=[
            pltpu.VMEM((2 * (last - 1), rows, width), BF16),
            pltpu.VMEM((rank, width), F32),
            pltpu.SemaphoreType.DMA,
            pltpu.SemaphoreType.DMA((2 + 2 * (last - 1) * tiles,)),
        ],
        compiler_params=pltpu.CompilerParams(vmem_limit_bytes=14 * MIB),
        cost_estimate=pl.CostEstimate(
            flops=4 * rank * rows * wid, bytes_accessed=2 * rows * wid, transcendentals=0
        ),
        name="update",
    )(place, columns, *pieces[1:], made, share, came, weight)
    return (new_weight[None], new_factor[None])


def solution(mesh):
    placed = (P("blk", "shard", None), P("blk", None, None))
    return jax.shard_map(
        on_device,
        mesh=mesh,
        in_specs=placed,
        out_specs=(P("blk", "shard", None), P("blk", None, "shard")),
        check_vma=False,
    )
```

```python
import functools

import jax
import jax.numpy as jnp
from jax import lax
from jax.experimental import pallas as pl
from jax.experimental.pallas import tpu as pltpu
from jax.sharding import PartitionSpec as P

POWER = 4
MIXING = 1.0 / 3.0
CHUNKS = 2
LANES = 128
PIVOTS = 4
TILE = 512
MIB = 1024 * 1024
F32 = jnp.float32
BF16 = jnp.bfloat16
HIGHEST = lax.Precision.HIGHEST
VMEM = pl.BlockSpec(memory_space=pltpu.VMEM)
SMEM = pl.BlockSpec(memory_space=pltpu.SMEM)
HBM = pl.BlockSpec(memory_space=pl.ANY)


def kernel_call(body, outs, name, *operands, scratch=(), mib=8, flops=0, moved=0):
    specs = []
    for operand in operands:
        specs.append(SMEM if operand.dtype == jnp.int32 else VMEM)
    return pl.pallas_call(
        body,
        out_shape=outs,
        in_specs=specs,
        out_specs=jax.tree.map(lambda _: VMEM, outs),
        scratch_shapes=list(scratch),
        compiler_params=pltpu.CompilerParams(vmem_limit_bytes=mib * MIB),
        cost_estimate=pl.CostEstimate(flops=flops, bytes_accessed=moved, transcendentals=0),
        name=name,
    )(*operands)


def out(shape, dtype):
    return jax.ShapeDtypeStruct(shape, dtype)


def hold_kernel(source, held, turned, sems):
    tile = source.shape[0] // sems.shape[0]
    spans = [slice(i * tile, (i + 1) * tile) for i in range(sems.shape[0])]
    copies = [
        pltpu.make_async_copy(source.at[span, :], held.at[span, :], sems.at[i])
        for i, span in enumerate(spans)
    ]
    for copy in copies:
        copy.start()
    for copy, span in zip(copies, spans):
        copy.wait()
        turned[:, span] = held[span, :].T


def hold(weight):
    rows, wid = weight.shape
    return pl.pallas_call(
        hold_kernel,
        out_shape=(pltpu.VMEM((rows, wid), weight.dtype), pltpu.VMEM((wid, rows), weight.dtype)),
        in_specs=[HBM],
        out_specs=(VMEM, VMEM),
        scratch_shapes=[pltpu.SemaphoreType.DMA((max(1, rows // 256),))],
        compiler_params=pltpu.CompilerParams(vmem_limit_bytes=32 * MIB),
        cost_estimate=pl.CostEstimate(flops=0, bytes_accessed=2 * rows * wid, transcendentals=0),
        name="hold",
    )(weight)


def first_kernel(chunk, place, own, prior, turned, even, odd, factor):
    rank, rows = even.shape
    parity = place[1]
    factor[pl.ds(pl.multiple_of(parity * rank, rank), rank), :] = own[...]
    factor[pl.ds(pl.multiple_of((1 - parity) * rank, rank), rank), :] = prior[...]
    product = jnp.dot(
        factor[...], turned[:, chunk * rows : (chunk + 1) * rows], preferred_element_type=F32
    )
    even[...] = product[:rank]
    odd[...] = product[rank:]


def slice_starts(place, offset, count, width, wid):
    low = jnp.bitwise_xor(jnp.bitwise_and(place[0], count - 1), offset) * width
    return pl.multiple_of(low, width), pl.multiple_of(low + wid // 2, width)


def piece_product(place, offset, count, piece, turned, columns):
    width = piece.shape[1] // 2
    low, high = slice_starts(place, offset, count, width, turned.shape[0])
    return jnp.dot(
        piece[:, :width], turned[pl.ds(low, width), columns], preferred_element_type=F32
    ) + jnp.dot(piece[:, width:], turned[pl.ds(high, width), columns], preferred_element_type=F32)


def own_kernel(count, place, piece, turned, partial):
    partial[...] = piece_product(place, 0, count, piece, turned, slice(None))


def next_kernel(chunk, place, *refs):
    *pieces, partial, turned, even, odd = refs
    rank, rows = even.shape
    columns = slice(chunk * rows, (chunk + 1) * rows)
    product = partial[:, columns]
    for offset, piece in enumerate(pieces, 1):
        product += piece_product(place, offset, len(pieces) + 1, piece, turned, columns)
    even[...] = product[:rank]
    odd[...] = product[rank:]


def chosen(place, bit):
    return jnp.bitwise_and(lax.div(place[0], jnp.int32(bit)), 1)


def split_raw(even, odd, even_other, odd_other, both):
    rank = even.shape[0]
    for slot, (mine, theirs) in enumerate(((even, even_other), (odd, odd_other))):
        raw = mine[...] - theirs[...]
        high = raw.astype(BF16)
        both[slot * rank : (slot + 1) * rank, :] = high
        both[(2 + slot) * rank : (3 + slot) * rank, :] = (raw - high.astype(F32)).astype(BF16)


def gram_of(both):
    rank = both.shape[0] // 4
    parts = lax.dot_general(
        both[...], both[...], (((1,), (1,)), ((), ())), preferred_element_type=F32
    )
    parts = parts[: 2 * rank] + parts[2 * rank :]
    parts = parts[:, : 2 * rank] + parts[:, 2 * rank :]
    gram = jnp.concatenate([parts[:rank, :rank], parts[rank:, rank:]], axis=0)
    return jnp.concatenate([gram, jnp.zeros((2 * rank, LANES - rank), F32)], axis=1)


def folded(product):
    rank2 = product.shape[0] // 2
    return product[:rank2] + product[rank2:]


def back_kernel(chunk, *refs):
    *products, weight, both, total, gram = refs
    rows = both.shape[1]
    split_raw(*products, both)
    total[...] = folded(
        jnp.dot(
            both[...], weight[chunk * rows : (chunk + 1) * rows, :], preferred_element_type=F32
        )
    )
    gram[...] = gram_of(both)


def half_product(wanted, slices, both, total, weight, result):
    rows = both.shape[1]
    width = weight.shape[1] // slices
    for i in range(slices // 2):
        columns = pl.ds(pl.multiple_of((2 * i + wanted) * width, width), width)
        product = jnp.dot(
            both[...], weight[weight.shape[0] - rows :, columns], preferred_element_type=F32
        )
        result[:, i * width : (i + 1) * width] = total[:, columns] + folded(product)


def back_send_kernel(slices, place, *refs):
    *products, total, gram, weight, both, send = refs
    split_raw(*products, both)
    half_product(1 - chosen(place, 1), slices, both, total, weight, send)
    send[:, -LANES:] = gram[...] + gram_of(both)


def back_keep_kernel(slices, place, both, total, weight, keep):
    half_product(chosen(place, 1), slices, both, total, weight, keep)


def merge_kernel(bit, slices, place, held, held_gram, came, keep, send):
    width = held.shape[1] // slices
    mine = chosen(place, bit)
    for i in range(slices // 2):
        kept = pl.ds(pl.multiple_of((2 * i + mine) * width, width), width)
        sent = pl.ds(pl.multiple_of((2 * i + 1 - mine) * width, width), width)
        keep[:, i * width : (i + 1) * width] = held[:, kept] + came[:, kept]
        send[:, i * width : (i + 1) * width] = held[:, sent] + came[:, sent]
    send[:, -LANES:] = held_gram[:, -LANES:] + came[:, -LANES:]


def add_kernel(held, held_gram, came, even, odd, gram):
    rank = even.shape[0]
    even[...] = held[:rank, :] + came[:rank, :-LANES]
    odd[...] = held[rank:, :] + came[rank:, :-LANES]
    gram[...] = held_gram[:, -LANES:] + came[:, -LANES:]


def inverse_kernel(gram, came, inverse):
    rank = gram.shape[0] // 2
    shape = (2, rank, LANES)
    lane = lax.broadcasted_iota(jnp.int32, shape, 2)
    row = lax.broadcasted_iota(jnp.int32, shape, 1)
    work = (gram[...] + came[...]).reshape(shape)
    work = jnp.where(lane < rank, work, jnp.where(lane - rank == row, 1.0, 0.0))
    for k in range(0, rank, PIVOTS):
        span = range(k, min(k + PIVOTS, rank))
        columns = [jnp.broadcast_to(work[:, :, j : j + 1], shape) for j in span]
        for i, j in enumerate(span):
            scale = 1.0 / columns[i][:, j : j + 1, :]
            below = jnp.where(row > j, columns[i], 0.0)
            work = work - below * (work[:, j : j + 1, :] * scale)
            for later in range(i + 1, len(columns)):
                other = columns[later]
                columns[later] = other - below * (other[:, j : j + 1, :] * scale)
    diagonal = jnp.sum(jnp.where(lane == row, work, 0.0), axis=2, keepdims=True)
    work = work / jnp.sqrt(diagonal)
    inverse[...] = work.reshape(2 * rank, LANES)[:, rank : 2 * rank]


def normalised(inverse, even, odd):
    rank = even.shape[0]
    return jnp.concatenate(
        [
            jnp.dot(inverse[:rank, :], even, precision=HIGHEST, preferred_element_type=F32),
            jnp.dot(inverse[rank:, :], odd, precision=HIGHEST, preferred_element_type=F32),
        ],
        axis=0,
    )


def share_kernel(inverse, even, odd, even_pair, odd_pair, share):
    value = normalised(inverse[...], even[...] + even_pair[...], odd[...] + odd_pair[...])
    share[...] = value.astype(share.dtype)


def blend_kernel(share, came, *refs):
    refs[-1][...] = (share[...].astype(F32) + came[...].astype(F32)).astype(BF16)


def slice_kernel(bit, place, inverse, even, odd, even_pair, odd_pair, own):
    rank, width = own.shape
    mine = pl.ds(pl.multiple_of(chosen(place, bit) * width, width), width)
    total = jnp.where(
        place[1] == 0, even[:, mine] + even_pair[:, mine], odd[:, mine] + odd_pair[:, mine]
    )
    lower = jnp.where(place[1] == 0, inverse[:rank, :], inverse[rank:, :])
    own[...] = jnp.dot(lower, total, precision=HIGHEST, preferred_element_type=F32)


def basis_kernel(inverse, *refs):
    *chunks, columns = refs
    for i, both in enumerate(chunks):
        rank2 = both.shape[0] // 2
        rows = both.shape[1]
        raw = both[:rank2, :].astype(F32) + both[rank2:, :].astype(F32)
        basis = normalised(inverse[...], raw[: rank2 // 2], raw[rank2 // 2 :])
        columns[i * rows : (i + 1) * rows, :] = basis.T.astype(BF16)


def updated(columns, piece, weight, rows, there, held):
    delta = jnp.dot(columns[rows, :], piece[:, held], preferred_element_type=F32)
    return (weight[rows, there].astype(F32) - MIXING * delta).astype(BF16)


def update_own_kernel(count, place, columns, piece, weight, made):
    rows, width = made.shape[1:]
    tile = min(TILE, rows)
    for j, start in enumerate(slice_starts(place, 0, count, width, weight.shape[1])):
        for first in range(0, rows, tile):
            span = slice(first, first + tile)
            held = slice(j * width, (j + 1) * width)
            made[j, span, :] = updated(columns, piece, weight, span, pl.ds(start, width), held)


def update_kernel(bit, count, place, columns, *refs):
    pieces = refs[: count - 1]
    own_made, factor, came, weight, result, own, made, value, own_sem, sems = refs[count - 1 :]
    rank, width = own.shape
    mine = pl.ds(pl.multiple_of(chosen(place, bit) * width, width), width)
    ours = pl.ds(pl.multiple_of(place[1] * rank, rank), rank)
    value[...] = factor[...] + came[ours, mine].astype(F32)
    copies = [pltpu.make_async_copy(value, own, own_sem)]
    copies[0].start()
    rows = weight.shape[0]

    def put(source, index, span, there):
        copy = pltpu.make_async_copy(source, result.at[span, there], sems.at[index])
        copy.start()
        copies.append(copy)

    index = 0
    for j, start in enumerate(slice_starts(place, 0, count, width, weight.shape[1])):
        put(own_made.at[j], index, slice(None), pl.ds(start, width))
        index += 1
    tile = rows // ((sems.shape[0] - 2) // (2 * (count - 1)))
    for i, piece in enumerate(pieces):
        for j, start in enumerate(slice_starts(place, i + 1, count, width, weight.shape[1])):
            there = pl.ds(start, width)
            held = slice(j * width, (j + 1) * width)
            for first in range(0, rows, tile):
                span = slice(first, first + tile)
                made[2 * i + j, span, :] = updated(columns, piece, weight, span, there, held)
                put(made.at[2 * i + j, span, :], index, span, there)
                index += 1
    for copy in copies:
        copy.wait()


def on_device(weights, warm_factor):
    peers = lax.axis_size("blk")
    shards = lax.axis_size("shard")
    shard = lax.axis_index("shard")
    parity = lax.rem(lax.axis_index("blk"), 2)
    place = jnp.stack([shard, parity]).astype(jnp.int32)
    bits = [1 << i for i in range(shards.bit_length() - 1)]
    last = bits[-1]
    partner = {
        0: [i + 1 if i % 2 == 0 else i - 1 for i in range(peers)],
        1: [(i + 1) % peers if i % 2 else (i - 1) % peers for i in range(peers)],
    }

    def across(value, bit):
        return lax.ppermute(value, "shard", [(i, i ^ bit) for i in range(shards)])

    def paired(value, slot):
        return lax.ppermute(value, "blk", list(enumerate(partner[slot])))

    own = warm_factor[0].astype(BF16)
    rank, wid = own.shape
    prior = lax.ppermute(own, "blk", [(i, (i + 1) % peers) for i in range(peers)])
    weight, turned = hold(weights[0])
    rows = weight.shape[0]
    width = wid // shards
    chunk_rows = rows // CHUNKS
    cost = dict(flops=4 * rank * chunk_rows * wid, moved=chunk_rows * wid * 2)
    product_outs = (out((rank, chunk_rows), F32), out((rank, chunk_rows), F32))
    factor_scratch = [pltpu.VMEM((2 * rank, wid), BF16)]
    gram_out = out((2 * rank, LANES), F32)
    both_out = out((4 * rank, chunk_rows), BF16)
    part_out = out((rank, 2 * width), F32)

    products = [
        kernel_call(
            functools.partial(first_kernel, chunk), product_outs, "first",
            place, own, prior, turned, scratch=factor_scratch, mib=8, **cost,
        )
        for chunk in range(CHUNKS)
    ]
    for iteration in range(POWER):
        final = iteration == POWER - 1
        even_other = paired(products[0][0], 0)
        odd_other = paired(products[0][1], 1)
        odd_last = paired(products[1][1], 1)
        even_last = paired(products[1][0], 0)
        exchanged = [(*products[0], even_other, odd_other), (*products[1], even_last, odd_last)]
        slices = shards
        half = slices // 2 * width
        both, total, gram = kernel_call(
            functools.partial(back_kernel, 0), (both_out, out((2 * rank, wid), F32), gram_out),
            "back", *exchanged[0], weight, mib=8, **cost,
        )
        both_last, send = kernel_call(
            functools.partial(back_send_kernel, slices),
            (both_out, out((2 * rank, half + LANES), F32)), "back_send",
            place, *exchanged[1], total, gram, weight, mib=8, **cost,
        )
        keep = kernel_call(
            functools.partial(back_keep_kernel, slices), out((2 * rank, half), F32), "back_keep",
            place, both_last, total, weight, mib=8, **cost,
        )
        gram = send
        for bit in bits[:-1]:
            came = across(send, bit)
            slices //= 2
            half = slices // 2 * width
            if 2 * bit == last:
                even, odd, gram = kernel_call(
                    add_kernel, (part_out, part_out, gram_out), "add", keep, gram, came
                )
                break
            keep, send = kernel_call(
                functools.partial(merge_kernel, 2 * bit, slices),
                (out((2 * rank, half), F32), out((2 * rank, half + LANES), F32)), "merge",
                place, keep, gram, came,
            )
            gram = send
        gram_came = across(gram, last)
        odd_pair = paired(odd, 1)
        even_pair = paired(even, 0)
        inverse = kernel_call(
            inverse_kernel, out((2 * rank, rank), F32), "inverse", gram, gram_came,
            flops=1000000, moved=8 * MIB,
        )
        share = kernel_call(
            share_kernel, out((2 * rank, 2 * width), BF16), "share",
            inverse, even, odd, even_pair, odd_pair,
        )
        came = across(share, last)
        if final:
            columns = kernel_call(
                basis_kernel, out((rows, 2 * rank), BF16), "basis", inverse, both, both_last,
                mib=8, flops=8 * rank * rank * rows, moved=2 * MIB,
            )
            factor = kernel_call(
                functools.partial(slice_kernel, last), out((rank, width), F32), "slice",
                place, inverse, even, odd, even_pair, odd_pair,
            )
        rounded = kernel_call(
            blend_kernel, out((2 * rank, 2 * width), BF16), "blend",
            share, came, *([columns, factor] if final else []),
        )
        pieces = {0: rounded}
        for bit in reversed(bits[:-1]):
            for offset in list(pieces):
                pieces[offset ^ bit] = across(pieces[offset], bit)
        pieces = [pieces[offset] for offset in range(last)]
        if not final:
            partial = kernel_call(
                functools.partial(own_kernel, last), out((2 * rank, rows), F32), "own",
                place, rounded, turned, mib=8, **cost,
            )
            products = [
                kernel_call(
                    functools.partial(next_kernel, chunk), product_outs, "next",
                    place, *pieces[1:], partial, turned, mib=8, **cost,
                )
                for chunk in range(CHUNKS)
            ]
    made = kernel_call(
        functools.partial(update_own_kernel, last), out((2, rows, width), BF16), "update_own",
        place, columns, rounded, weight, mib=8, flops=8 * rank * rows * width, moved=6 * rows * width,
    )
    tiles = max(1, rows // TILE)
    new_weight, new_factor = pl.pallas_call(
        functools.partial(update_kernel, last, last),
        out_shape=(out((rows, wid), BF16), out((rank, width), F32)),
        in_specs=[SMEM] + [VMEM] * (last + 4),
        out_specs=(HBM, HBM),
        scratch_shapes=[
            pltpu.VMEM((2 * (last - 1), rows, width), BF16),
            pltpu.VMEM((rank, width), F32),
            pltpu.SemaphoreType.DMA,
            pltpu.SemaphoreType.DMA((2 + 2 * (last - 1) * tiles,)),
        ],
        compiler_params=pltpu.CompilerParams(vmem_limit_bytes=14 * MIB),
        cost_estimate=pl.CostEstimate(
            flops=4 * rank * rows * wid, bytes_accessed=2 * rows * wid, transcendentals=0
        ),
        name="update",
    )(place, columns, *pieces[1:], made, factor, came, weight)
    return (new_weight[None], new_factor[None])


def solution(mesh):
    placed = (P("blk", "shard", None), P("blk", None, None))
    return jax.shard_map(
        on_device,
        mesh=mesh,
        in_specs=placed,
        out_specs=(P("blk", "shard", None), P("blk", None, "shard")),
        check_vma=False,
    )
```

```python
import functools

import jax
import jax.numpy as jnp
from jax import lax
from jax.experimental import pallas as pl
from jax.experimental.pallas import tpu as pltpu
from jax.sharding import PartitionSpec as P

POWER = 4
MIXING = 1.0 / 3.0
CHUNKS = 2
FIRST_EIGHTHS = 5
LANES = 128
PIVOTS = 4
TILE = 512
MIB = 1024 * 1024
F32 = jnp.float32
BF16 = jnp.bfloat16
HIGHEST = lax.Precision.HIGHEST
VMEM = pl.BlockSpec(memory_space=pltpu.VMEM)
SMEM = pl.BlockSpec(memory_space=pltpu.SMEM)
HBM = pl.BlockSpec(memory_space=pl.ANY)


def kernel_call(body, outs, name, *operands, scratch=(), mib=8, flops=0, moved=0):
    specs = []
    for operand in operands:
        specs.append(SMEM if operand.dtype == jnp.int32 else VMEM)
    return pl.pallas_call(
        body,
        out_shape=outs,
        in_specs=specs,
        out_specs=jax.tree.map(lambda _: VMEM, outs),
        scratch_shapes=list(scratch),
        compiler_params=pltpu.CompilerParams(vmem_limit_bytes=mib * MIB),
        cost_estimate=pl.CostEstimate(flops=flops, bytes_accessed=moved, transcendentals=0),
        name=name,
    )(*operands)


def out(shape, dtype):
    return jax.ShapeDtypeStruct(shape, dtype)


def hold_kernel(source, held, turned, sems):
    tile = source.shape[0] // sems.shape[0]
    spans = [slice(i * tile, (i + 1) * tile) for i in range(sems.shape[0])]
    copies = [
        pltpu.make_async_copy(source.at[span, :], held.at[span, :], sems.at[i])
        for i, span in enumerate(spans)
    ]
    for copy in copies:
        copy.start()
    for copy, span in zip(copies, spans):
        copy.wait()
        turned[:, span] = held[span, :].T


def hold(weight):
    rows, wid = weight.shape
    return pl.pallas_call(
        hold_kernel,
        out_shape=(pltpu.VMEM((rows, wid), weight.dtype), pltpu.VMEM((wid, rows), weight.dtype)),
        in_specs=[HBM],
        out_specs=(VMEM, VMEM),
        scratch_shapes=[pltpu.SemaphoreType.DMA((max(1, rows // 256),))],
        compiler_params=pltpu.CompilerParams(vmem_limit_bytes=32 * MIB),
        cost_estimate=pl.CostEstimate(flops=0, bytes_accessed=2 * rows * wid, transcendentals=0),
        name="hold",
    )(weight)


def chunk_span(chunk, rows, whole):
    return slice(0, rows) if chunk == 0 else slice(whole - rows, whole)


def first_kernel(chunk, place, own, prior, turned, even, odd, factor):
    rank, rows = even.shape
    parity = place[1]
    factor[pl.ds(pl.multiple_of(parity * rank, rank), rank), :] = own[...]
    factor[pl.ds(pl.multiple_of((1 - parity) * rank, rank), rank), :] = prior[...]
    product = jnp.dot(
        factor[...], turned[:, chunk_span(chunk, rows, turned.shape[1])], preferred_element_type=F32
    )
    even[...] = product[:rank]
    odd[...] = product[rank:]


def slice_starts(place, offset, count, width, wid):
    low = jnp.bitwise_xor(jnp.bitwise_and(place[0], count - 1), offset) * width
    return pl.multiple_of(low, width), pl.multiple_of(low + wid // 2, width)


def piece_product(place, offset, count, piece, turned, columns):
    width = piece.shape[1] // 2
    low, high = slice_starts(place, offset, count, width, turned.shape[0])
    return jnp.dot(
        piece[:, :width], turned[pl.ds(low, width), columns], preferred_element_type=F32
    ) + jnp.dot(piece[:, width:], turned[pl.ds(high, width), columns], preferred_element_type=F32)


def own_kernel(count, place, piece, turned, partial):
    partial[...] = piece_product(place, 0, count, piece, turned, slice(None))


def next_kernel(chunk, place, *refs):
    *pieces, partial, turned, even, odd = refs
    rank, rows = even.shape
    columns = chunk_span(chunk, rows, turned.shape[1])
    product = partial[:, columns]
    for offset, piece in enumerate(pieces, 1):
        product += piece_product(place, offset, len(pieces) + 1, piece, turned, columns)
    even[...] = product[:rank]
    odd[...] = product[rank:]


def chosen(place, bit):
    return jnp.bitwise_and(lax.div(place[0], jnp.int32(bit)), 1)


def split_raw(even, odd, even_other, odd_other, both):
    rank = even.shape[0]
    for slot, (mine, theirs) in enumerate(((even, even_other), (odd, odd_other))):
        raw = mine[...] - theirs[...]
        high = raw.astype(BF16)
        both[slot * rank : (slot + 1) * rank, :] = high
        both[(2 + slot) * rank : (3 + slot) * rank, :] = (raw - high.astype(F32)).astype(BF16)


def gram_of(both):
    rank = both.shape[0] // 4
    parts = lax.dot_general(
        both[...], both[...], (((1,), (1,)), ((), ())), preferred_element_type=F32
    )
    parts = parts[: 2 * rank] + parts[2 * rank :]
    parts = parts[:, : 2 * rank] + parts[:, 2 * rank :]
    gram = jnp.concatenate([parts[:rank, :rank], parts[rank:, rank:]], axis=0)
    return jnp.concatenate([gram, jnp.zeros((2 * rank, LANES - rank), F32)], axis=1)


def folded(product):
    rank2 = product.shape[0] // 2
    return product[:rank2] + product[rank2:]


def back_kernel(chunk, *refs):
    *products, weight, both, total, gram = refs
    rows = both.shape[1]
    split_raw(*products, both)
    total[...] = folded(
        jnp.dot(
            both[...], weight[chunk_span(chunk, rows, weight.shape[0]), :], preferred_element_type=F32
        )
    )
    gram[...] = gram_of(both)


def half_product(wanted, slices, both, total, weight, result):
    rows = both.shape[1]
    width = weight.shape[1] // slices
    for i in range(slices // 2):
        columns = pl.ds(pl.multiple_of((2 * i + wanted) * width, width), width)
        product = jnp.dot(
            both[...], weight[weight.shape[0] - rows :, columns], preferred_element_type=F32
        )
        result[:, i * width : (i + 1) * width] = total[:, columns] + folded(product)


def back_send_kernel(slices, place, *refs):
    *products, total, gram, weight, both, send = refs
    split_raw(*products, both)
    half_product(1 - chosen(place, 1), slices, both, total, weight, send)
    send[:, -LANES:] = gram[...] + gram_of(both)


def back_keep_kernel(slices, place, both, total, weight, keep):
    half_product(chosen(place, 1), slices, both, total, weight, keep)


def merge_kernel(bit, slices, place, held, held_gram, came, keep, send):
    width = held.shape[1] // slices
    mine = chosen(place, bit)
    for i in range(slices // 2):
        kept = pl.ds(pl.multiple_of((2 * i + mine) * width, width), width)
        sent = pl.ds(pl.multiple_of((2 * i + 1 - mine) * width, width), width)
        keep[:, i * width : (i + 1) * width] = held[:, kept] + came[:, kept]
        send[:, i * width : (i + 1) * width] = held[:, sent] + came[:, sent]
    send[:, -LANES:] = held_gram[:, -LANES:] + came[:, -LANES:]


def add_kernel(held, held_gram, came, even, odd, gram):
    rank = even.shape[0]
    even[...] = held[:rank, :] + came[:rank, :-LANES]
    odd[...] = held[rank:, :] + came[rank:, :-LANES]
    gram[...] = held_gram[:, -LANES:] + came[:, -LANES:]


def inverse_kernel(gram, came, inverse):
    rank = gram.shape[0] // 2
    shape = (2, rank, LANES)
    lane = lax.broadcasted_iota(jnp.int32, shape, 2)
    row = lax.broadcasted_iota(jnp.int32, shape, 1)
    work = (gram[...] + came[...]).reshape(shape)
    work = jnp.where(lane < rank, work, jnp.where(lane - rank == row, 1.0, 0.0))
    for k in range(0, rank, PIVOTS):
        span = range(k, min(k + PIVOTS, rank))
        columns = [jnp.broadcast_to(work[:, :, j : j + 1], shape) for j in span]
        for i, j in enumerate(span):
            scale = 1.0 / columns[i][:, j : j + 1, :]
            below = jnp.where(row > j, columns[i], 0.0)
            work = work - below * (work[:, j : j + 1, :] * scale)
            for later in range(i + 1, len(columns)):
                other = columns[later]
                columns[later] = other - below * (other[:, j : j + 1, :] * scale)
    diagonal = jnp.sum(jnp.where(lane == row, work, 0.0), axis=2, keepdims=True)
    work = work / jnp.sqrt(diagonal)
    inverse[...] = work.reshape(2 * rank, LANES)[:, rank : 2 * rank]


def normalised(inverse, even, odd):
    rank = even.shape[0]
    return jnp.concatenate(
        [
            jnp.dot(inverse[:rank, :], even, precision=HIGHEST, preferred_element_type=F32),
            jnp.dot(inverse[rank:, :], odd, precision=HIGHEST, preferred_element_type=F32),
        ],
        axis=0,
    )


def share_kernel(inverse, even, odd, even_pair, odd_pair, share):
    value = normalised(inverse[...], even[...] + even_pair[...], odd[...] + odd_pair[...])
    share[...] = value.astype(share.dtype)


def blend_kernel(share, came, *refs):
    refs[-1][...] = (share[...].astype(F32) + came[...].astype(F32)).astype(BF16)


def slice_kernel(bit, place, inverse, even, odd, even_pair, odd_pair, own):
    rank, width = own.shape
    mine = pl.ds(pl.multiple_of(chosen(place, bit) * width, width), width)
    total = jnp.where(
        place[1] == 0, even[:, mine] + even_pair[:, mine], odd[:, mine] + odd_pair[:, mine]
    )
    lower = jnp.where(place[1] == 0, inverse[:rank, :], inverse[rank:, :])
    own[...] = jnp.dot(lower, total, precision=HIGHEST, preferred_element_type=F32)


def basis_kernel(inverse, *refs):
    *chunks, columns = refs
    start = 0
    for both in chunks:
        rank2 = both.shape[0] // 2
        rows = both.shape[1]
        raw = both[:rank2, :].astype(F32) + both[rank2:, :].astype(F32)
        basis = normalised(inverse[...], raw[: rank2 // 2], raw[rank2 // 2 :])
        columns[start : start + rows, :] = basis.T.astype(BF16)
        start += rows


def updated(columns, piece, weight, rows, there, held):
    delta = jnp.dot(columns[rows, :], piece[:, held], preferred_element_type=F32)
    return (weight[rows, there].astype(F32) - MIXING * delta).astype(BF16)


def update_own_kernel(count, place, columns, piece, weight, made):
    rows, width = made.shape[1:]
    tile = min(TILE, rows)
    for j, start in enumerate(slice_starts(place, 0, count, width, weight.shape[1])):
        for first in range(0, rows, tile):
            span = slice(first, first + tile)
            held = slice(j * width, (j + 1) * width)
            made[j, span, :] = updated(columns, piece, weight, span, pl.ds(start, width), held)


def update_kernel(bit, count, place, columns, *refs):
    pieces = refs[: count - 1]
    own_made, factor, came, weight, result, own, made, value, own_sem, sems = refs[count - 1 :]
    rank, width = own.shape
    mine = pl.ds(pl.multiple_of(chosen(place, bit) * width, width), width)
    ours = pl.ds(pl.multiple_of(place[1] * rank, rank), rank)
    value[...] = factor[...] + came[ours, mine].astype(F32)
    copies = [pltpu.make_async_copy(value, own, own_sem)]
    copies[0].start()
    rows = weight.shape[0]

    def put(source, index, span, there):
        copy = pltpu.make_async_copy(source, result.at[span, there], sems.at[index])
        copy.start()
        copies.append(copy)

    index = 0
    for j, start in enumerate(slice_starts(place, 0, count, width, weight.shape[1])):
        put(own_made.at[j], index, slice(None), pl.ds(start, width))
        index += 1
    tile = rows // ((sems.shape[0] - 2) // (2 * (count - 1)))
    for i, piece in enumerate(pieces):
        for j, start in enumerate(slice_starts(place, i + 1, count, width, weight.shape[1])):
            there = pl.ds(start, width)
            held = slice(j * width, (j + 1) * width)
            for first in range(0, rows, tile):
                span = slice(first, first + tile)
                made[2 * i + j, span, :] = updated(columns, piece, weight, span, there, held)
                put(made.at[2 * i + j, span, :], index, span, there)
                index += 1
    for copy in copies:
        copy.wait()


def on_device(weights, warm_factor):
    peers = lax.axis_size("blk")
    shards = lax.axis_size("shard")
    shard = lax.axis_index("shard")
    parity = lax.rem(lax.axis_index("blk"), 2)
    place = jnp.stack([shard, parity]).astype(jnp.int32)
    bits = [1 << i for i in range(shards.bit_length() - 1)]
    last = bits[-1]
    partner = {
        0: [i + 1 if i % 2 == 0 else i - 1 for i in range(peers)],
        1: [(i + 1) % peers if i % 2 else (i - 1) % peers for i in range(peers)],
    }

    def across(value, bit):
        return lax.ppermute(value, "shard", [(i, i ^ bit) for i in range(shards)])

    def paired(value, slot):
        return lax.ppermute(value, "blk", list(enumerate(partner[slot])))

    own = warm_factor[0].astype(BF16)
    rank, wid = own.shape
    prior = lax.ppermute(own, "blk", [(i, (i + 1) % peers) for i in range(peers)])
    weight, turned = hold(weights[0])
    rows = weight.shape[0]
    width = wid // shards
    first_rows = rows * FIRST_EIGHTHS // 8 // LANES * LANES
    chunks = (first_rows, rows - first_rows)
    cost = dict(flops=2 * rank * rows * wid, moved=rows * wid)
    product_outs = [(out((rank, chunk), F32),) * 2 for chunk in chunks]
    factor_scratch = [pltpu.VMEM((2 * rank, wid), BF16)]
    gram_out = out((2 * rank, LANES), F32)
    both_outs = [out((4 * rank, chunk), BF16) for chunk in chunks]
    part_out = out((rank, 2 * width), F32)

    products = [
        kernel_call(
            functools.partial(first_kernel, chunk), product_outs[chunk], "first",
            place, own, prior, turned, scratch=factor_scratch, mib=8, **cost,
        )
        for chunk in range(CHUNKS)
    ]
    for iteration in range(POWER):
        final = iteration == POWER - 1
        even_other = paired(products[0][0], 0)
        odd_other = paired(products[0][1], 1)
        odd_last = paired(products[1][1], 1)
        even_last = paired(products[1][0], 0)
        exchanged = [(*products[0], even_other, odd_other), (*products[1], even_last, odd_last)]
        slices = shards
        half = slices // 2 * width
        both, total, gram = kernel_call(
            functools.partial(back_kernel, 0), (both_outs[0], out((2 * rank, wid), F32), gram_out),
            "back", *exchanged[0], weight, mib=8, **cost,
        )
        both_last, send = kernel_call(
            functools.partial(back_send_kernel, slices),
            (both_outs[1], out((2 * rank, half + LANES), F32)), "back_send",
            place, *exchanged[1], total, gram, weight, mib=8, **cost,
        )
        keep = kernel_call(
            functools.partial(back_keep_kernel, slices), out((2 * rank, half), F32), "back_keep",
            place, both_last, total, weight, mib=8, **cost,
        )
        gram = send
        for bit in bits[:-1]:
            came = across(send, bit)
            slices //= 2
            half = slices // 2 * width
            if 2 * bit == last:
                even, odd, gram = kernel_call(
                    add_kernel, (part_out, part_out, gram_out), "add", keep, gram, came
                )
                break
            keep, send = kernel_call(
                functools.partial(merge_kernel, 2 * bit, slices),
                (out((2 * rank, half), F32), out((2 * rank, half + LANES), F32)), "merge",
                place, keep, gram, came,
            )
            gram = send
        gram_came = across(gram, last)
        odd_pair = paired(odd, 1)
        even_pair = paired(even, 0)
        inverse = kernel_call(
            inverse_kernel, out((2 * rank, rank), F32), "inverse", gram, gram_came,
            flops=1000000, moved=8 * MIB,
        )
        share = kernel_call(
            share_kernel, out((2 * rank, 2 * width), BF16), "share",
            inverse, even, odd, even_pair, odd_pair,
        )
        came = across(share, last)
        if final:
            columns = kernel_call(
                basis_kernel, out((rows, 2 * rank), BF16), "basis", inverse, both, both_last,
                mib=8, flops=8 * rank * rank * rows, moved=2 * MIB,
            )
            factor = kernel_call(
                functools.partial(slice_kernel, last), out((rank, width), F32), "slice",
                place, inverse, even, odd, even_pair, odd_pair,
            )
        rounded = kernel_call(
            blend_kernel, out((2 * rank, 2 * width), BF16), "blend",
            share, came, *([columns, factor] if final else []),
        )
        pieces = {0: rounded}
        for bit in reversed(bits[:-1]):
            for offset in list(pieces):
                pieces[offset ^ bit] = across(pieces[offset], bit)
        pieces = [pieces[offset] for offset in range(last)]
        if not final:
            partial = kernel_call(
                functools.partial(own_kernel, last), out((2 * rank, rows), F32), "own",
                place, rounded, turned, mib=8, **cost,
            )
            products = [
                kernel_call(
                    functools.partial(next_kernel, chunk), product_outs[chunk], "next",
                    place, *pieces[1:], partial, turned, mib=8, **cost,
                )
                for chunk in range(CHUNKS)
            ]
    made = kernel_call(
        functools.partial(update_own_kernel, last), out((2, rows, width), BF16), "update_own",
        place, columns, rounded, weight, mib=8, flops=8 * rank * rows * width, moved=6 * rows * width,
    )
    tiles = max(1, rows // TILE)
    new_weight, new_factor = pl.pallas_call(
        functools.partial(update_kernel, last, last),
        out_shape=(out((rows, wid), BF16), out((rank, width), F32)),
        in_specs=[SMEM] + [VMEM] * (last + 4),
        out_specs=(HBM, HBM),
        scratch_shapes=[
            pltpu.VMEM((2 * (last - 1), rows, width), BF16),
            pltpu.VMEM((rank, width), F32),
            pltpu.SemaphoreType.DMA,
            pltpu.SemaphoreType.DMA((2 + 2 * (last - 1) * tiles,)),
        ],
        compiler_params=pltpu.CompilerParams(vmem_limit_bytes=14 * MIB),
        cost_estimate=pl.CostEstimate(
            flops=4 * rank * rows * wid, bytes_accessed=2 * rows * wid, transcendentals=0
        ),
        name="update",
    )(place, columns, *pieces[1:], made, factor, came, weight)
    return (new_weight[None], new_factor[None])


def solution(mesh):
    placed = (P("blk", "shard", None), P("blk", None, None))
    return jax.shard_map(
        on_device,
        mesh=mesh,
        in_specs=placed,
        out_specs=(P("blk", "shard", None), P("blk", None, "shard")),
        check_vma=False,
    )
```
